32 devices in a mesh: ctx: 4 (over y, x), chan: 8 (over z, core).
Axes of the slice: x: 2, y: 2, z: 4, core: 2. Of those that a mesh axis runs over, the one named last changes fastest.
Arguments:
- tokens: bfloat16 [2048, 4096], P('ctx', 'chan'), may hold values from -7 to 7
- in_proj: bfloat16 [3, 4096, 4096], P(None, 'chan'), may hold values from -0.125 to 0.125
- short_taps: float32 [3, 4096, 3], P(None, 'chan'), may hold values from -3.5 to 3.5
- long_filter: bfloat16 [4096, 2048], P('chan', 'ctx'), may hold values from -1.3 to 1.3
- skip_gain: float32 [4096], P('chan'), may hold values from -4 to 4
Outputs:
- gated: bfloat16 [4096, 2048], P('chan', 'ctx')
The draws below stay inside these ranges and needn't reach their ends.
All inputs are finite; a program needn't handle non-finite values.
Results may differ from the reference program's by a relative error of at most 0.0075.
Values may be sent and summed in bfloat16 or wider, within the bound.
No kernel may reach another device: no remote copies, remote signals or barrier semaphores. Data moves between devices by JAX's collectives and lax.ppermute only.
A program may use at most 192 MiB of HBM per device.

```python
import math
import jax
import jax.numpy as jnp
from jax import lax

D = 4096
TOKENS = 2048


def draw_tokens(key, part):
    key = jax.random.fold_in(key, 11)
    keys = jax.random.split(key, 2)
    offset = 0.4 * jnp.clip(jax.random.normal(keys[0], (D,), jnp.float32), -2.5, 2.5)
    noise = jnp.clip(jax.random.normal(keys[1], (TOKENS, D), jnp.float32), -6.0, 6.0)
    return (noise + offset[None, :]).astype(jnp.bfloat16)


def draw_long_filter(key, part):
    key = jax.random.fold_in(key, 7)
    keys = jax.random.split(key, 8)
    time_points = jnp.arange(TOKENS, dtype=jnp.float32)
    share = 0.5
    random_jitter = jnp.clip(jax.random.normal(keys[0], (D, TOKENS), jnp.float32), -4.0, 4.0)
    slow = jax.random.uniform(keys[1], (D,), jnp.float32) < share
    long_span = TOKENS * jnp.exp(jax.random.uniform(keys[2], (D,), jnp.float32, math.log(0.5), math.log(4.0)))
    short_span = jnp.exp(jax.random.uniform(keys[3], (D,), jnp.float32, math.log(10.0), math.log(40.0)))
    span_lengths = jnp.where(slow, long_span, short_span)
    place_indices = jax.random.randint(keys[4], (4,), 0, TOKENS)
    dropped_entries = jnp.log(jax.random.uniform(keys[5], (4,), jnp.float32, 0.5, 0.8))
    pulse_train = jnp.sum(jnp.where(time_points[None, :] >= place_indices[:, None].astype(jnp.float32), dropped_entries[:, None], 0.0), axis=0)
    plateau_sign = jnp.where(jax.random.uniform(keys[6], (D,), jnp.float32) < 0.5, -1.0, 1.0)
    roughness = 0.5 + jax.random.uniform(keys[7], (D, TOKENS), jnp.float32)
    far_lags = jnp.logical_not(slow)[:, None] & (time_points[None, :] > 4.0 * span_lengths[:, None])
    tail_values = jnp.where(far_lags, 0.0005 * plateau_sign[:, None] * roughness, 0.0)
    scale_factor = 1.0 / jnp.sqrt(jnp.minimum(span_lengths, float(TOKENS)))
    head_values = random_jitter * jnp.exp(-time_points[None, :] / span_lengths[:, None])
    value_entries = scale_factor[:, None] * (head_values + tail_values) * jnp.exp(pulse_train[None, :])
    return value_entries.astype(jnp.bfloat16)


def raised(entries, stream_key, source, target, shards_of, factor):
    owner, partner = [(jnp.arange(entries.shape[dim]) // (entries.shape[dim] // shards_of)).reshape([-1 if axis == dim else 1 for axis in range(entries.ndim)]) for dim in (source, target)]
    chosen = jax.random.permutation(stream_key, shards_of)[partner]
    strong = (owner == chosen) | (owner == (partner + shards_of // 2) % shards_of)
    return jnp.where(strong, factor * entries, entries)


def levels(rng, shape, shards, smallest, top_value):
    level = 1.0
    for dim, shards_of in shards:
        heights = jax.random.uniform(jax.random.fold_in(jax.random.fold_in(rng, 6), dim), (shards_of,), jnp.float32, smallest / len(shards), top_value / len(shards))
        level = level * jnp.repeat(jnp.exp(heights), shape[dim] // shards_of).reshape((-1,) + (1,) * (len(shape) - 1 - dim))
    return level


def centred(stream_key, extent, width, most, shards=(), kind=jnp.bfloat16):
    level = levels(stream_key, extent, shards, -0.22, 0.18) if shards else 1.0
    array = jax.random.normal(stream_key, extent, jnp.float32) * width * level
    return jnp.minimum(jnp.maximum(array, -most), most).astype(kind)


def noise_with(key, extent, scale, most, shards, heavy, kind=jnp.bfloat16):
    result = scale * jax.random.normal(key, extent, jnp.float32)
    if shards:
        result = result * levels(key, extent, shards, -0.22, 0.18)
    return jnp.clip(raised(result, jax.random.fold_in(key, 3), *heavy), -most, most).astype(kind)


def setup_inputs(seed: int = 0) -> dict:
    streams_of = jax.random.split(jax.random.key(seed), 6)
    return {
        "tokens": draw_tokens(jax.random.fold_in(streams_of[5], 71), 0),
        "in_proj": noise_with(streams_of[1], (3, D, D), D ** -0.5, 0.125, ((1, 8),), (1, 2, 8, 2.0)),
        "short_taps": centred(streams_of[2], (3, D, 3), 3 ** -0.5, 3.5, ((1, 8),), jnp.float32),
        "long_filter": draw_long_filter(jax.random.fold_in(streams_of[5], 71), 0),
        "skip_gain": centred(streams_of[4], (D,), 1.0, 4.0, ((0, 8),), jnp.float32),
    }


def reference(tokens, in_proj, short_taps, long_filter, skip_gain):
    summed = jnp.einsum("td,kdc->kct", tokens.astype(jnp.float32), in_proj.astype(jnp.float32), precision=lax.Precision.HIGHEST)
    rounded = lax.optimization_barrier(summed.astype(jnp.bfloat16))
    mixed = rounded.astype(jnp.float32)
    padded = jnp.pad(mixed, ((0, 0), (0, 0), (2, 0)))
    featured = short_taps[:, :, 0:1] * padded[:, :, 2:] + short_taps[:, :, 1:2] * padded[:, :, 1:TOKENS + 1] + short_taps[:, :, 2:3] * padded[:, :, 0:TOKENS]
    product = (featured[1] * featured[2]).astype(jnp.bfloat16)
    signal = product.astype(jnp.float32)
    kernel = long_filter.astype(jnp.float32)
    length = 2 * TOKENS
    spectrum = jnp.fft.rfft(signal, length, axis=1) * jnp.fft.rfft(kernel, length, axis=1)
    convolved = jnp.fft.irfft(spectrum, length, axis=1)[:, :TOKENS]
    answer = convolved + skip_gain[:, None] * signal
    return (featured[0] * answer).astype(jnp.bfloat16)
```

```python
import functools

import jax
import jax.numpy as jnp
import ml_dtypes
import numpy as np
from jax import lax
from jax.experimental import pallas as pl
from jax.experimental.pallas import tpu as pltpu
from jax.sharding import PartitionSpec as P

VMEM_LIMIT = 48 * 1024 * 1024
F32 = jnp.float32
BF16 = jnp.bfloat16


def wave_tables(length):
    position = np.arange(length, dtype=np.int64)
    phase = (position[:, None] * (2 * position[None, :] + 1)) % (4 * length)
    angle = phase.astype(np.float64) * (2.0 * np.pi / (4 * length))
    table = np.concatenate([np.cos(angle), -np.sin(angle)], axis=1)
    high = table.astype(ml_dtypes.bfloat16)
    low = (table - high.astype(np.float64)).astype(ml_dtypes.bfloat16)
    return high, low


def spectrum(values, high, low):
    return jnp.dot(values, high, preferred_element_type=F32) + jnp.dot(
        values, low, preferred_element_type=F32
    )


def filter_kernel(taps_ref, high_ref, low_ref, out_ref):
    blocks, rows, length = taps_ref.shape
    values = taps_ref[...].reshape(blocks * rows, length)
    waves = spectrum(values, high_ref[...], low_ref[...]) * (1.0 / length)
    lane = lax.broadcasted_iota(jnp.int32, (rows, length), 1)
    sign = jnp.where(lane % 2 == 0, 1.0, -1.0)
    for m in range(blocks):
        real = waves[m * rows : (m + 1) * rows, :length]
        imag = waves[m * rows : (m + 1) * rows, length:]
        if m:
            real = real - sign * waves[(m - 1) * rows : m * rows, length:]
            imag = imag + sign * waves[(m - 1) * rows : m * rows, :length]
        out_ref[m, :, :length] = real
        out_ref[m, :, length:] = imag


def filter_waves(moved_filter, high, low):
    blocks, rows, length = moved_filter.shape
    step = min(rows, 64)
    return pl.pallas_call(
        filter_kernel,
        grid=(rows // step,),
        in_specs=[
            pl.BlockSpec((blocks, step, length), lambda g: (0, g, 0)),
            pl.BlockSpec((length, 2 * length), lambda g: (0, 0)),
            pl.BlockSpec((length, 2 * length), lambda g: (0, 0)),
        ],
        out_specs=pl.BlockSpec((blocks, step, 2 * length), lambda g: (0, g, 0)),
        out_shape=jax.ShapeDtypeStruct((blocks, rows, 2 * length), F32),
        compiler_params=pltpu.CompilerParams(vmem_limit_bytes=VMEM_LIMIT),
        name="filter_waves",
    )(moved_filter, high, low)


def feature(own, other, taps):
    mixed = (own + other).astype(BF16).astype(F32)
    lane = lax.broadcasted_iota(jnp.int32, mixed.shape, 1)
    one = jnp.where(lane >= 1, pltpu.roll(mixed, 1, 1), 0.0)
    two = jnp.where(lane >= 2, pltpu.roll(mixed, 2, 1), 0.0)
    return taps[:, 0:1] * mixed + taps[:, 1:2] * one + taps[:, 2:3] * two


def conv_kernel(own_ref, other_ref, taps_ref, skip_ref, waves_ref, high_ref, low_ref, out_ref):
    blocks, rows, double = waves_ref.shape
    length = double // 2
    product = (
        feature(own_ref[0], other_ref[0], taps_ref[1]) * feature(own_ref[1], other_ref[1], taps_ref[2])
    ).astype(BF16)
    values = jnp.concatenate(
        [product[:, p * length : (p + 1) * length] for p in range(blocks)], axis=0
    )
    high = high_ref[...]
    low = low_ref[...]
    waves = spectrum(values, high, low)
    pieces = []
    for p in range(blocks):
        real = jnp.zeros((rows, length), F32)
        imag = jnp.zeros((rows, length), F32)
        for q in range(p + 1):
            in_real = waves[q * rows : (q + 1) * rows, :length]
            in_imag = waves[q * rows : (q + 1) * rows, length:]
            tap_real = waves_ref[p - q, :, :length]
            tap_imag = waves_ref[p - q, :, length:]
            real = real + (in_real * tap_real - in_imag * tap_imag)
            imag = imag + (in_real * tap_imag + in_imag * tap_real)
        pieces.append(jnp.concatenate([real, imag], axis=1))
    total = jnp.concatenate(pieces, axis=0)
    total_high = total.astype(BF16)
    total_low = (total - total_high.astype(F32)).astype(BF16)
    dims = (((1,), (1,)), ((), ()))
    back = (
        lax.dot_general(total_high, high, dims, preferred_element_type=F32)
        + lax.dot_general(total_low, high, dims, preferred_element_type=F32)
        + lax.dot_general(total_high, low, dims, preferred_element_type=F32)
    )
    skip = skip_ref[...]
    for p in range(blocks):
        span = slice(p * length, (p + 1) * length)
        out_ref[:, span] = back[p * rows : (p + 1) * rows] + skip * product[:, span].astype(F32)


def convolve(own, other, taps, skip, waves, high, low):
    streams, rows, span = own.shape
    blocks, _, double = waves.shape
    step = min(rows, 64)
    return pl.pallas_call(
        conv_kernel,
        grid=(rows // step,),
        in_specs=[
            pl.BlockSpec((streams, step, span), lambda g: (0, g, 0)),
            pl.BlockSpec((streams, step, span), lambda g: (0, g, 0)),
            pl.BlockSpec((3, step, 3), lambda g: (0, g, 0)),
            pl.BlockSpec((step, 1), lambda g: (g, 0)),
            pl.BlockSpec((blocks, step, double), lambda g: (0, g, 0)),
            pl.BlockSpec((double // 2, double), lambda g: (0, 0)),
            pl.BlockSpec((double // 2, double), lambda g: (0, 0)),
        ],
        out_specs=pl.BlockSpec((step, span), lambda g: (g, 0)),
        out_shape=jax.ShapeDtypeStruct((rows, span), F32),
        compiler_params=pltpu.CompilerParams(vmem_limit_bytes=VMEM_LIMIT),
        name="convolve",
    )(own, other, taps, skip, waves, high, low)


def gate_kernel(own_ref, other_ref, taps_ref, answer_ref, out_ref):
    blocks, _, length = out_ref.shape
    gated = (feature(own_ref[...], other_ref[...], taps_ref[0]) * answer_ref[...]).astype(BF16)
    for p in range(blocks):
        out_ref[p] = gated[:, p * length : (p + 1) * length]


def gate(own, other, taps, answer, blocks):
    rows, span = own.shape
    step = min(rows, 64)
    return pl.pallas_call(
        gate_kernel,
        grid=(rows // step,),
        in_specs=[
            pl.BlockSpec((step, span), lambda g: (g, 0)),
            pl.BlockSpec((step, span), lambda g: (g, 0)),
            pl.BlockSpec((3, step, 3), lambda g: (0, g, 0)),
            pl.BlockSpec((step, span), lambda g: (g, 0)),
        ],
        out_specs=pl.BlockSpec((blocks, step, span // blocks), lambda g: (0, g, 0)),
        out_shape=jax.ShapeDtypeStruct((blocks, rows, span // blocks), BF16),
        compiler_params=pltpu.CompilerParams(vmem_limit_bytes=VMEM_LIMIT),
        name="gate",
    )(own, other, taps, answer)


def swap(x, axis, bit):
    return lax.ppermute(x, axis, [(i, i ^ bit) for i in range(lax.axis_size(axis))])


def gather_context(block):
    size = lax.axis_size("ctx")
    if size != 4:
        return lax.all_gather(block, "ctx", axis=1, tiled=True)
    me = lax.axis_index("ctx")
    groups, length, depth = block.shape
    half = length // 2
    near = swap(block, "ctx", 1)
    far = swap(block, "ctx", 2)
    first = swap(far[:, :half], "ctx", 1)
    second = swap(near[:, half:], "ctx", 2)
    whole = jnp.zeros((groups, size * length, depth), block.dtype)
    for piece, row in (
        (block, me * length),
        (near, (me ^ 1) * length),
        (far, (me ^ 2) * length),
        (first, (me ^ 3) * length),
        (second, (me ^ 3) * length + half),
    ):
        whole = lax.dynamic_update_slice(whole, piece, (0, row, 0))
    return whole


def gather_features(block):
    size = lax.axis_size("chan")
    chips = size // 2
    place = lax.axis_index("chan") // 2
    left, right = [], []
    up, down = block, block
    for _ in range(1, chips):
        up = lax.ppermute(up, "chan", [(i, i + 2) for i in range(size - 2)])
        down = lax.ppermute(down, "chan", [(i + 2, i) for i in range(size - 2)])
        left.append(up)
        right.append(down)
    return jnp.stack(
        [jnp.where(place >= s, left[s - 1], right[chips - s - 1]) for s in range(1, chips)]
    )


def body(tokens, in_proj, short_taps, long_filter, skip_gain):
    length, _ = tokens.shape
    cycle = lax.axis_size("ctx")
    size = lax.axis_size("chan")
    chips = size // 2
    me = lax.axis_index("ctx")
    place = lax.axis_index("chan") // 2
    core = lax.axis_index("chan") % 2
    few = in_proj.shape[2] // (size * cycle)
    high, low = (jnp.asarray(t) for t in wave_tables(length))

    def columns(s, streams):
        owner = (place + s) % chips
        parts = []
        for side in range(2):
            start = ((2 * owner + (core ^ side)) * cycle + me) * few
            for k in streams:
                parts.append(lax.dynamic_slice_in_dim(in_proj[k], start, few, axis=1))
        return jnp.concatenate(parts, axis=1)

    def travel(piece, s):
        pairs = [(i, (i + 2 * s) % size) for i in range(size)]
        return lax.ppermute(piece, "chan", pairs)

    moved_filter = lax.all_to_all(
        long_filter.reshape(cycle, few, length), "ctx", split_axis=0, concat_axis=0, tiled=True
    )
    waves = filter_waves(moved_filter, high, low)

    others = gather_features(tokens)
    own_tokens = gather_context(tokens[None])[0]
    other_tokens = gather_context(others)

    def project(streams):
        total = None
        for s in range(chips):
            piece = columns(s, streams)
            if s:
                piece = travel(piece, s)
            these = own_tokens if s == 0 else other_tokens[s - 1]
            part = jnp.einsum("td,dc->ct", these, piece, preferred_element_type=F32)
            total = part if total is None else total + part
        rows = len(streams) * few
        return total[:rows], swap(total[rows:], "chan", 1)

    own_taps = lax.dynamic_slice_in_dim(short_taps, me * few, few, axis=1)
    own_skip = lax.dynamic_slice_in_dim(skip_gain, me * few, few)[:, None]
    span = own_tokens.shape[0]
    mine, theirs = project((1, 2))
    answer = convolve(
        mine.reshape(2, few, span), theirs.reshape(2, few, span), own_taps, own_skip, waves, high, low
    )
    mine, theirs = project((0,))
    gated = gate(mine, theirs, own_taps, answer, cycle)
    moved = lax.all_to_all(gated, "ctx", split_axis=0, concat_axis=0, tiled=True)
    return moved.reshape(cycle * few, length)


def solution(mesh):
    in_specs = (
        P("ctx", "chan"),
        P(None, "chan", None),
        P(None, "chan", None),
        P("chan", "ctx"),
        P("chan"),
    )
    out_specs = P("chan", "ctx")
    return jax.shard_map(body, mesh=mesh, in_specs=in_specs, out_specs=out_specs, check_vma=False)
```

```python
import functools

import jax
import jax.numpy as jnp
import ml_dtypes
import numpy as np
from jax import lax
from jax.experimental import pallas as pl
from jax.experimental.pallas import tpu as pltpu
from jax.sharding import PartitionSpec as P

VMEM_LIMIT = 32 * 1024 * 1024
PROJECT_LIMIT = 60 * 1024 * 1024
F32 = jnp.float32
BF16 = jnp.bfloat16


def wave_tables(length):
    position = np.arange(length, dtype=np.int64)
    phase = (position[:, None] * (2 * position[None, :] + 1)) % (4 * length)
    angle = phase.astype(np.float64) * (2.0 * np.pi / (4 * length))
    table = np.concatenate([np.cos(angle), -np.sin(angle)], axis=1)
    high = table.astype(ml_dtypes.bfloat16)
    low = (table - high.astype(np.float64)).astype(ml_dtypes.bfloat16)
    return high, low


def spectrum(values, high, low):
    return jnp.dot(values, high, preferred_element_type=F32) + jnp.dot(
        values, low, preferred_element_type=F32
    )


def filter_kernel(taps_ref, high_ref, low_ref, out_ref):
    blocks, rows, length = taps_ref.shape
    values = taps_ref[...].reshape(blocks * rows, length)
    waves = spectrum(values, high_ref[...], low_ref[...]) * (1.0 / length)
    lane = lax.broadcasted_iota(jnp.int32, (rows, length), 1)
    sign = jnp.where(lane % 2 == 0, 1.0, -1.0)
    for m in range(blocks):
        real = waves[m * rows : (m + 1) * rows, :length]
        imag = waves[m * rows : (m + 1) * rows, length:]
        if m:
            real = real - sign * waves[(m - 1) * rows : m * rows, length:]
            imag = imag + sign * waves[(m - 1) * rows : m * rows, :length]
        out_ref[m, :, :length] = real
        out_ref[m, :, length:] = imag


def filter_waves(moved_filter, high, low):
    blocks, rows, length = moved_filter.shape
    step = min(rows, 64)
    return pl.pallas_call(
        filter_kernel,
        grid=(rows // step,),
        in_specs=[
            pl.BlockSpec((blocks, step, length), lambda g: (0, g, 0)),
            pl.BlockSpec((length, 2 * length), lambda g: (0, 0)),
            pl.BlockSpec((length, 2 * length), lambda g: (0, 0)),
        ],
        out_specs=pl.BlockSpec((blocks, step, 2 * length), lambda g: (0, g, 0)),
        out_shape=jax.ShapeDtypeStruct((blocks, rows, 2 * length), F32),
        compiler_params=pltpu.CompilerParams(vmem_limit_bytes=VMEM_LIMIT),
        name="filter_waves",
    )(moved_filter, high, low)


def feature(own, other, taps):
    mixed = (own + other).astype(BF16).astype(F32)
    lane = lax.broadcasted_iota(jnp.int32, mixed.shape, 1)
    one = jnp.where(lane >= 1, pltpu.roll(mixed, 1, 1), 0.0)
    two = jnp.where(lane >= 2, pltpu.roll(mixed, 2, 1), 0.0)
    return taps[:, 0:1] * mixed + taps[:, 1:2] * one + taps[:, 2:3] * two


def conv_kernel(own_ref, other_ref, taps_ref, skip_ref, waves_ref, high_ref, low_ref, out_ref):
    blocks, rows, double = waves_ref.shape
    length = double // 2
    product = (
        feature(own_ref[0], other_ref[0], taps_ref[1]) * feature(own_ref[1], other_ref[1], taps_ref[2])
    ).astype(BF16)
    values = jnp.concatenate(
        [product[:, p * length : (p + 1) * length] for p in range(blocks)], axis=0
    )
    high = high_ref[...]
    low = low_ref[...]
    waves = spectrum(values, high, low)
    pieces = []
    for p in range(blocks):
        real = jnp.zeros((rows, length), F32)
        imag = jnp.zeros((rows, length), F32)
        for q in range(p + 1):
            in_real = waves[q * rows : (q + 1) * rows, :length]
            in_imag = waves[q * rows : (q + 1) * rows, length:]
            tap_real = waves_ref[p - q, :, :length]
            tap_imag = waves_ref[p - q, :, length:]
            real = real + (in_real * tap_real - in_imag * tap_imag)
            imag = imag + (in_real * tap_imag + in_imag * tap_real)
        pieces.append(jnp.concatenate([real, imag], axis=1))
    total = jnp.concatenate(pieces, axis=0)
    total_high = total.astype(BF16)
    total_low = (total - total_high.astype(F32)).astype(BF16)
    dims = (((1,), (1,)), ((), ()))
    back = (
        lax.dot_general(total_high, high, dims, preferred_element_type=F32)
        + lax.dot_general(total_low, high, dims, preferred_element_type=F32)
        + lax.dot_general(total_high, low, dims, preferred_element_type=F32)
    )
    skip = skip_ref[...]
    for p in range(blocks):
        span = slice(p * length, (p + 1) * length)
        out_ref[:, span] = back[p * rows : (p + 1) * rows] + skip * product[:, span].astype(F32)


def convolve(own, other, taps, skip, waves, high, low):
    streams, rows, span = own.shape
    blocks, _, double = waves.shape
    step = min(rows, 64)
    return pl.pallas_call(
        conv_kernel,
        grid=(rows // step,),
        in_specs=[
            pl.BlockSpec((streams, step, span), lambda g: (0, g, 0)),
            pl.BlockSpec((streams, step, span), lambda g: (0, g, 0)),
            pl.BlockSpec((3, step, 3), lambda g: (0, g, 0)),
            pl.BlockSpec((step, 1), lambda g: (g, 0)),
            pl.BlockSpec((blocks, step, double), lambda g: (0, g, 0)),
            pl.BlockSpec((double // 2, double), lambda g: (0, 0)),
            pl.BlockSpec((double // 2, double), lambda g: (0, 0)),
        ],
        out_specs=pl.BlockSpec((step, span), lambda g: (g, 0)),
        out_shape=jax.ShapeDtypeStruct((rows, span), F32),
        compiler_params=pltpu.CompilerParams(vmem_limit_bytes=VMEM_LIMIT),
        name="convolve",
    )(own, other, taps, skip, waves, high, low)


def gate_kernel(own_ref, other_ref, taps_ref, answer_ref, out_ref):
    blocks, _, length = out_ref.shape
    gated = (feature(own_ref[...], other_ref[...], taps_ref[0]) * answer_ref[...]).astype(BF16)
    for p in range(blocks):
        out_ref[p] = gated[:, p * length : (p + 1) * length]


def gate(own, other, taps, answer, blocks):
    rows, span = own.shape
    step = min(rows, 64)
    return pl.pallas_call(
        gate_kernel,
        grid=(rows // step,),
        in_specs=[
            pl.BlockSpec((step, span), lambda g: (g, 0)),
            pl.BlockSpec((step, span), lambda g: (g, 0)),
            pl.BlockSpec((3, step, 3), lambda g: (0, g, 0)),
            pl.BlockSpec((step, span), lambda g: (g, 0)),
        ],
        out_specs=pl.BlockSpec((blocks, step, span // blocks), lambda g: (0, g, 0)),
        out_shape=jax.ShapeDtypeStruct((blocks, rows, span // blocks), BF16),
        compiler_params=pltpu.CompilerParams(vmem_limit_bytes=VMEM_LIMIT),
        name="gate",
    )(own, other, taps, answer)


def swap(x, axis, bit):
    return lax.ppermute(x, axis, [(i, i ^ bit) for i in range(lax.axis_size(axis))])


def pick_kernel(at_ref, in_proj_ref, *refs):
    chips = len(refs) // 2
    few = in_proj_ref.shape[2]
    for s in range(chips):

        @pl.when(pl.program_id(0) // 2 == s)
        def _():
            refs[s][:, :few] = in_proj_ref[1]
            refs[s][:, few:] = in_proj_ref[2]
            refs[chips + s][...] = in_proj_ref[0]


def pick_columns(in_proj, chips, few, place, core, me, cycle):
    depth = in_proj.shape[1]
    order = [2 * (place ^ s) + (core ^ side) for s in range(chips) for side in range(2)]
    at = jnp.stack([o * cycle + me for o in order]).astype(jnp.int32)
    if few % 128:
        parts = [
            [lax.dynamic_slice_in_dim(in_proj[k], at[n] * few, few, axis=1) for n in range(2 * chips)]
            for k in range(3)
        ]
        pairs = [
            jnp.concatenate([parts[k][2 * s + side] for side in range(2) for k in (1, 2)], axis=1)
            for s in range(chips)
        ]
        singles = [jnp.concatenate(parts[0][2 * s : 2 * s + 2], axis=1) for s in range(chips)]
        return pairs, singles

    def target(s):
        return lambda g, at: (0, jnp.clip(g - 2 * s, 0, 1))

    outs = pl.pallas_call(
        pick_kernel,
        grid_spec=pltpu.PrefetchScalarGridSpec(
            num_scalar_prefetch=1,
            grid=(2 * chips,),
            in_specs=[pl.BlockSpec((3, depth, few), lambda g, at: (0, 0, at[g]))],
            out_specs=[pl.BlockSpec((depth, 2 * few), target(s)) for s in range(chips)]
            + [pl.BlockSpec((depth, few), target(s)) for s in range(chips)],
        ),
        out_shape=[jax.ShapeDtypeStruct((depth, 4 * few), BF16)] * chips
        + [jax.ShapeDtypeStruct((depth, 2 * few), BF16)] * chips,
        compiler_params=pltpu.CompilerParams(vmem_limit_bytes=VMEM_LIMIT),
        name="pick_columns",
    )(at, in_proj)
    return outs[:chips], outs[chips:]


def swap_far(block):
    return swap(block, "ctx", 1), swap(block, "ctx", 2)


def move_chips(x, pairs):
    return lax.ppermute(x, "chan", [(2 * a + k, 2 * b + k) for a, b in pairs for k in range(2)])


def turn_chips(x, s):
    return move_chips(x, [(z, z ^ s) for z in range(lax.axis_size("chan") // 2)])


def gather(block, pairs, singles, long_filter, move_filter, make_waves):
    place = lax.axis_index("chan") // 2
    middle = [(1, 2), (2, 1)]
    ends = [(1, 0), (2, 3)]
    inner = (place == 1) | (place == 2)
    order = lax.optimization_barrier
    pairs, singles = list(pairs), list(singles)
    length = block.shape[0]
    half = length // 2

    def spread(near, far, own):
        if near is None:
            return swap_far(own)
        skip = near.shape[0] - length
        to_near, to_far = far[skip : skip + half], near[skip + half :]
        if own is not None:
            to_near, to_far = jnp.concatenate([to_near, own]), jnp.concatenate([to_far, own])
        return swap(to_near, "ctx", 1), swap(to_far, "ctx", 2)

    pair = move_chips(block, [(0, 1), (1, 0), (2, 3), (3, 2)])
    across = move_chips(block, middle)
    near0, far0 = spread(None, None, block)
    pair, across, near0, far0, pairs, singles, long_filter = order(
        (pair, across, near0, far0, pairs, singles, long_filter)
    )

    farther = move_chips(pair, middle)
    second = move_chips(across, ends)
    near1, far1 = spread(near0, far0, pair)
    pairs[3] = turn_chips(pairs[3], 3)
    pair_3 = pairs.pop()
    farther, second, near1, far1, pairs, singles, long_filter = order(
        (farther, second, near1, far1, pairs, singles, long_filter)
    )

    second = jnp.where(inner, across, second)
    third = move_chips(farther, ends)
    near2, far2 = spread(near1, far1, second)
    pair_2 = turn_chips(pairs[2], 2)
    moved_filter = move_filter(long_filter)
    third, near2, far2, pair_3, pairs, singles, moved_filter = order(
        (third, near2, far2, pair_3, pairs, singles, moved_filter)
    )

    third = jnp.where(inner, farther, third)
    near3, far3 = spread(near2, far2, third)
    pair_1 = turn_chips(pairs[1], 1)
    single_3 = turn_chips(singles[3], 3)
    waves = make_waves(moved_filter)
    near3, far3, pair_2, pair_1, singles, waves = order(
        (near3, far3, pair_2, pair_1, singles, waves)
    )

    near4, far4 = spread(near3, far3, None)
    single_1, single_2 = turn_chips(singles[1], 1), turn_chips(singles[2], 2)
    pairs = [pairs[0], pair_1, pair_2, pair_3]
    singles = [singles[0], single_1, single_2, single_3]
    slots = (
        [block, pair, second, third],
        [near0, near1, near2, near3, near4],
        [far0, far1, far2, far3, far4],
    )
    return slots, pairs, singles, waves


def gather_plain(block, pairs, singles, long_filter, move_filter, make_waves):
    chips = lax.axis_size("chan") // 2
    slots = [turn_chips(block, s) if s else block for s in range(chips)]
    pairs, singles = (
        [turn_chips(x, s) if s else x for s, x in enumerate(w)] for w in (pairs, singles)
    )
    return slots, pairs, singles, make_waves(move_filter(long_filter))


def project_kernel(plan, which, arrays, adds, at_ref, *refs):
    weights_refs, refs = refs[:4], refs[4:]
    pieces, refs = refs[:arrays], refs[arrays:]
    sums, (own_ref, other_ref, weights, values, weight_sems, sems) = refs[: 2 * adds], refs[2 * adds :]
    rows = own_ref.shape[0]
    length = values.shape[1] // 4
    weight_copies = [
        pltpu.make_async_copy(weights_refs[s], weights.at[s], weight_sems.at[s]) for s in range(4)
    ]
    copies = [
        [
            pltpu.make_async_copy(
                pieces[array].at[pl.ds(start, count)],
                values.at[s, pl.ds(target, count)],
                sems.at[5 * s + n],
            )
            for n, (array, start, count, target) in enumerate(plan[s])
        ]
        for s in range(len(plan))
    ]
    for copy in weight_copies:
        copy.start()
    for slot in copies:
        for copy in slot:
            copy.start()
    for copy in weight_copies:
        copy.wait()
    for s in range(len(plan)):
        turned = weights[at_ref[4 + which[s]]].T
        for copy in copies[s]:
            copy.wait()
        for q in range(4):
            part = lax.dot_general(
                turned,
                values[s, q * length : (q + 1) * length],
                (((1,), (1,)), ((), ())),
                preferred_element_type=F32,
            )
            span = pl.ds(pl.multiple_of(at_ref[q], length), length)
            if s:
                own_ref[:, span] += part[:rows]
                other_ref[:, span] += part[rows:]
            elif adds:
                own_ref[:, span] = sums[0][:, span] + part[:rows]
                other_ref[:, span] = sums[1][:, span] + part[rows:]
            else:
                own_ref[:, span] = part[:rows]
                other_ref[:, span] = part[rows:]


def project_plain(slots, weights):
    total = 0.0
    for block, piece in zip(slots, weights):
        full = lax.all_gather(block, "ctx", axis=0, tiled=True)
        total = total + jnp.einsum("td,dc->ct", full, piece, preferred_element_type=F32)
    rows = total.shape[0] // 2
    return total[:rows], total[rows:]


def project(slots, weights, first, last, sums=()):
    blocks, near, far = slots
    length, depth = blocks[0].shape
    half = length // 2
    rows = weights[0].shape[1] // 2
    me = lax.axis_index("ctx")
    place = lax.axis_index("chan") // 2
    swapped = jnp.where((place == 1) | (place == 2), 1, 0)
    at = jnp.stack([(me ^ q) * length for q in range(4)] + [0 * me, 0 * me + 1, 2 + swapped, 3 - swapped])
    arrays, plan = [], []

    def place_of(x):
        for n, y in enumerate(arrays):
            if y is x:
                return n
        arrays.append(x)
        return len(arrays) - 1

    for s in range(first, last):
        skip = half if s else 0
        plan.append(
            (
                (place_of(blocks[s]), 0, length, 0),
                (place_of(near[s]), skip, length, length),
                (place_of(far[s]), skip, length, 2 * length),
                (place_of(near[s + 1]), 0, half, 3 * length),
                (place_of(far[s + 1]), 0, half, 3 * length + half),
            )
        )
    out = jax.ShapeDtypeStruct((rows, 4 * length), F32)
    spec = pl.BlockSpec((rows, 4 * length), lambda g, at: (0, 0))
    return pl.pallas_call(
        functools.partial(project_kernel, plan, range(first, last), len(arrays), len(sums) // 2),
        grid_spec=pltpu.PrefetchScalarGridSpec(
            num_scalar_prefetch=1,
            grid=(1,),
            in_specs=[pl.BlockSpec(memory_space=pl.ANY)] * (4 + len(arrays)) + [spec] * len(sums),
            out_specs=[spec] * 2,
            scratch_shapes=[
                pltpu.VMEM((4, *weights[0].shape), BF16),
                pltpu.VMEM((last - first, 4 * length, depth), BF16),
                pltpu.SemaphoreType.DMA((4,)),
                pltpu.SemaphoreType.DMA((5 * (last - first),)),
            ],
        ),
        out_shape=[out, out],
        compiler_params=pltpu.CompilerParams(vmem_limit_bytes=PROJECT_LIMIT),
        name="project",
    )(at.astype(jnp.int32), *weights, *arrays, *sums)


def body(tokens, in_proj, short_taps, long_filter, skip_gain):
    length, depth = tokens.shape
    cycle = lax.axis_size("ctx")
    size = lax.axis_size("chan")
    chips = size // 2
    me = lax.axis_index("ctx")
    place = lax.axis_index("chan") // 2
    core = lax.axis_index("chan") % 2
    few = in_proj.shape[2] // (size * cycle)
    span = length * cycle
    high, low = (jnp.asarray(t) for t in wave_tables(length))
    pairs, singles = pick_columns(in_proj, chips, few, place, core, me, cycle)
    fits = cycle == 4 and chips == 4 and length % 512 == 0 and depth % 128 == 0

    def move_filter(values):
        return lax.all_to_all(
            values.reshape(cycle, few, length), "ctx", split_axis=0, concat_axis=0, tiled=True
        )

    def make_waves(moved):
        return filter_waves(moved, high, low)

    slots, pairs, singles, waves = (gather if fits else gather_plain)(
        tokens, pairs, singles, long_filter, move_filter, make_waves
    )
    own_taps = lax.dynamic_slice_in_dim(short_taps, me * few, few, axis=1)
    own_skip = lax.dynamic_slice_in_dim(skip_gain, me * few, few)[:, None]
    if fits:
        sums, singles = lax.optimization_barrier((project(slots, pairs, 0, 3), singles))
        mine, send = project(slots, pairs, 3, 4, sums)
    else:
        mine, send = project_plain(slots, pairs)
    theirs = swap(send, "chan", 1)
    answer = convolve(
        mine.reshape(2, few, span), theirs.reshape(2, few, span), own_taps, own_skip, waves, high, low
    )
    mine, send = project(slots, singles, 0, 4) if fits else project_plain(slots, singles)
    gated = gate(mine, swap(send, "chan", 1), own_taps, answer, cycle)
    moved = lax.all_to_all(gated, "ctx", split_axis=0, concat_axis=0, tiled=True)
    return moved.reshape(cycle * few, length)


def solution(mesh):
    in_specs = (
        P("ctx", "chan"),
        P(None, "chan", None),
        P(None, "chan", None),
        P("chan", "ctx"),
        P("chan"),
    )
    out_specs = P("chan", "ctx")
    return jax.shard_map(body, mesh=mesh, in_specs=in_specs, out_specs=out_specs, check_vma=False)
```

```python
import functools

import jax
import jax.numpy as jnp
import ml_dtypes
import numpy as np
from jax import lax
from jax.experimental import pallas as pl
from jax.experimental.pallas import tpu as pltpu
from jax.sharding import PartitionSpec as P

VMEM_LIMIT = 32 * 1024 * 1024
PROJECT_LIMIT = 60 * 1024 * 1024
F32 = jnp.float32
BF16 = jnp.bfloat16


def wave_tables(length):
    position = np.arange(length, dtype=np.int64)
    phase = (position[:, None] * (2 * position[None, :] + 1)) % (4 * length)
    angle = phase.astype(np.float64) * (2.0 * np.pi / (4 * length))
    table = np.concatenate([np.cos(angle), -np.sin(angle)], axis=1)
    high = table.astype(ml_dtypes.bfloat16)
    low = (table - high.astype(np.float64)).astype(ml_dtypes.bfloat16)
    return high, low


def spectrum(values, high, low):
    return jnp.dot(values, high, preferred_element_type=F32) + jnp.dot(
        values, low, preferred_element_type=F32
    )


def filter_kernel(taps_ref, high_ref, low_ref, out_ref):
    blocks, rows, length = taps_ref.shape
    values = taps_ref[...].reshape(blocks * rows, length)
    waves = spectrum(values, high_ref[...], low_ref[...]) * (1.0 / length)
    lane = lax.broadcasted_iota(jnp.int32, (rows, length), 1)
    sign = jnp.where(lane % 2 == 0, 1.0, -1.0)
    for m in range(blocks):
        real = waves[m * rows : (m + 1) * rows, :length]
        imag = waves[m * rows : (m + 1) * rows, length:]
        if m:
            real = real - sign * waves[(m - 1) * rows : m * rows, length:]
            imag = imag + sign * waves[(m - 1) * rows : m * rows, :length]
        out_ref[m, :, :length] = real
        out_ref[m, :, length:] = imag


def filter_waves(moved_filter, high, low):
    blocks, rows, length = moved_filter.shape
    step = min(rows, 64)
    return pl.pallas_call(
        filter_kernel,
        grid=(rows // step,),
        in_specs=[
            pl.BlockSpec((blocks, step, length), lambda g: (0, g, 0)),
            pl.BlockSpec((length, 2 * length), lambda g: (0, 0)),
            pl.BlockSpec((length, 2 * length), lambda g: (0, 0)),
        ],
        out_specs=pl.BlockSpec((blocks, step, 2 * length), lambda g: (0, g, 0)),
        out_shape=jax.ShapeDtypeStruct((blocks, rows, 2 * length), F32),
        compiler_params=pltpu.CompilerParams(vmem_limit_bytes=VMEM_LIMIT),
        name="filter_waves",
    )(moved_filter, high, low)


def feature(own, other, taps):
    mixed = (own + other.astype(F32)).astype(BF16).astype(F32)
    lane = lax.broadcasted_iota(jnp.int32, mixed.shape, 1)
    one = jnp.where(lane >= 1, pltpu.roll(mixed, 1, 1), 0.0)
    two = jnp.where(lane >= 2, pltpu.roll(mixed, 2, 1), 0.0)
    return taps[:, 0:1] * mixed + taps[:, 1:2] * one + taps[:, 2:3] * two


def conv_kernel(own_ref, other_ref, taps_ref, skip_ref, waves_ref, high_ref, low_ref, out_ref):
    blocks, rows, double = waves_ref.shape
    length = double // 2
    product = (
        feature(own_ref[0], other_ref[0], taps_ref[1]) * feature(own_ref[1], other_ref[1], taps_ref[2])
    ).astype(BF16)
    values = jnp.concatenate(
        [product[:, p * length : (p + 1) * length] for p in range(blocks)], axis=0
    )
    high = high_ref[...]
    low = low_ref[...]
    waves = spectrum(values, high, low)
    pieces = []
    for p in range(blocks):
        real = jnp.zeros((rows, length), F32)
        imag = jnp.zeros((rows, length), F32)
        for q in range(p + 1):
            in_real = waves[q * rows : (q + 1) * rows, :length]
            in_imag = waves[q * rows : (q + 1) * rows, length:]
            tap_real = waves_ref[p - q, :, :length]
            tap_imag = waves_ref[p - q, :, length:]
            real = real + (in_real * tap_real - in_imag * tap_imag)
            imag = imag + (in_real * tap_imag + in_imag * tap_real)
        pieces.append(jnp.concatenate([real, imag], axis=1))
    total = jnp.concatenate(pieces, axis=0)
    total_high = total.astype(BF16)
    total_low = (total - total_high.astype(F32)).astype(BF16)
    dims = (((1,), (1,)), ((), ()))
    back = (
        lax.dot_general(total_high, high, dims, preferred_element_type=F32)
        + lax.dot_general(total_low, high, dims, preferred_element_type=F32)
        + lax.dot_general(total_high, low, dims, preferred_element_type=F32)
    )
    skip = skip_ref[...]
    for p in range(blocks):
        span = slice(p * length, (p + 1) * length)
        out_ref[:, span] = back[p * rows : (p + 1) * rows] + skip * product[:, span].astype(F32)


def convolve(own, other, taps, skip, waves, high, low):
    streams, rows, span = own.shape
    blocks, _, double = waves.shape
    step = min(rows, 64)
    return pl.pallas_call(
        conv_kernel,
        grid=(rows // step,),
        in_specs=[
            pl.BlockSpec((streams, step, span), lambda g: (0, g, 0)),
            pl.BlockSpec((streams, step, span), lambda g: (0, g, 0)),
            pl.BlockSpec((3, step, 3), lambda g: (0, g, 0)),
            pl.BlockSpec((step, 1), lambda g: (g, 0)),
            pl.BlockSpec((blocks, step, double), lambda g: (0, g, 0)),
            pl.BlockSpec((double // 2, double), lambda g: (0, 0)),
            pl.BlockSpec((double // 2, double), lambda g: (0, 0)),
        ],
        out_specs=pl.BlockSpec((step, span), lambda g: (g, 0)),
        out_shape=jax.ShapeDtypeStruct((rows, span), F32),
        compiler_params=pltpu.CompilerParams(vmem_limit_bytes=PROJECT_LIMIT),
        name="convolve",
    )(own, other, taps, skip, waves, high, low)


def gate_kernel(own_ref, other_ref, taps_ref, answer_ref, out_ref):
    blocks, _, length = out_ref.shape
    gated = (feature(own_ref[...], other_ref[...], taps_ref[0]) * answer_ref[...]).astype(BF16)
    for p in range(blocks):
        out_ref[p] = gated[:, p * length : (p + 1) * length]


def gate(own, other, taps, answer, blocks):
    rows, span = own.shape
    step = min(rows, 64)
    return pl.pallas_call(
        gate_kernel,
        grid=(rows // step,),
        in_specs=[
            pl.BlockSpec((step, span), lambda g: (g, 0)),
            pl.BlockSpec((step, span), lambda g: (g, 0)),
            pl.BlockSpec((3, step, 3), lambda g: (0, g, 0)),
            pl.BlockSpec((step, span), lambda g: (g, 0)),
        ],
        out_specs=pl.BlockSpec((blocks, step, span // blocks), lambda g: (0, g, 0)),
        out_shape=jax.ShapeDtypeStruct((blocks, rows, span // blocks), BF16),
        compiler_params=pltpu.CompilerParams(vmem_limit_bytes=VMEM_LIMIT),
        name="gate",
    )(own, other, taps, answer)


def swap(x, axis, bit):
    return lax.ppermute(x, axis, [(i, i ^ bit) for i in range(lax.axis_size(axis))])


def pick_kernel(at_ref, in_proj_ref, *refs):
    chips = len(refs) // 2
    few = in_proj_ref.shape[2]
    for s in range(chips):

        @pl.when(pl.program_id(0) // 2 == s)
        def _():
            refs[s][:, :few] = in_proj_ref[1]
            refs[s][:, few:] = in_proj_ref[2]
            refs[chips + s][...] = in_proj_ref[0]


def pick_columns(in_proj, chips, few, place, core, me, cycle):
    depth = in_proj.shape[1]
    order = [2 * (place ^ s) + (core ^ side) for s in range(chips) for side in range(2)]
    at = jnp.stack([o * cycle + me for o in order]).astype(jnp.int32)
    if few % 128:
        parts = [
            [lax.dynamic_slice_in_dim(in_proj[k], at[n] * few, few, axis=1) for n in range(2 * chips)]
            for k in range(3)
        ]
        pairs = [
            jnp.concatenate([parts[k][2 * s + side] for side in range(2) for k in (1, 2)], axis=1)
            for s in range(chips)
        ]
        singles = [jnp.concatenate(parts[0][2 * s : 2 * s + 2], axis=1) for s in range(chips)]
        return pairs, singles

    def target(s):
        return lambda g, at: (0, jnp.clip(g - 2 * s, 0, 1))

    outs = pl.pallas_call(
        pick_kernel,
        grid_spec=pltpu.PrefetchScalarGridSpec(
            num_scalar_prefetch=1,
            grid=(2 * chips,),
            in_specs=[pl.BlockSpec((3, depth, few), lambda g, at: (0, 0, at[g]))],
            out_specs=[pl.BlockSpec((depth, 2 * few), target(s)) for s in range(chips)]
            + [pl.BlockSpec((depth, few), target(s)) for s in range(chips)],
        ),
        out_shape=[jax.ShapeDtypeStruct((depth, 4 * few), BF16)] * chips
        + [jax.ShapeDtypeStruct((depth, 2 * few), BF16)] * chips,
        compiler_params=pltpu.CompilerParams(vmem_limit_bytes=PROJECT_LIMIT),
        name="pick_columns",
    )(at, in_proj)
    return outs[:chips], outs[chips:]


def swap_far(block):
    return swap(block, "ctx", 1), swap(block, "ctx", 2)


def move_chips(x, pairs):
    return lax.ppermute(x, "chan", [(2 * a + k, 2 * b + k) for a, b in pairs for k in range(2)])


def turn_chips(x, s):
    return move_chips(x, [(z, z ^ s) for z in range(lax.axis_size("chan") // 2)])


def gather(block, pairs, singles, long_filter, early):
    place = lax.axis_index("chan") // 2
    middle = [(1, 2), (2, 1)]
    ends = [(1, 0), (2, 3)]
    inner = (place == 1) | (place == 2)
    order = lax.optimization_barrier
    pairs, singles = list(pairs), list(singles)
    length = block.shape[0]
    half = length // 2

    def spread(to_near, to_far):
        return swap(jnp.concatenate(to_near), "ctx", 1), swap(jnp.concatenate(to_far), "ctx", 2)

    pair = move_chips(block, [(0, 1), (1, 0), (2, 3), (3, 2)])
    across = move_chips(block, middle)
    near0, far0 = swap_far(block)
    pair, across, near0, far0, pairs, singles, long_filter = order(
        (pair, across, near0, far0, pairs, singles, long_filter)
    )

    farther = move_chips(pair, middle)
    second = move_chips(across, ends)
    near1, far1 = swap_far(pair)
    pairs[3] = turn_chips(pairs[3], 3)
    pair_3 = pairs.pop()
    farther, second, near1, far1, pairs, singles, long_filter = order(
        (farther, second, near1, far1, pairs, singles, long_filter)
    )

    second = jnp.where(inner, across, second)
    third = move_chips(farther, ends)
    near2, far2 = spread(
        [far0[:half], far1[:half], second], [near0[half:], near1[half:], second]
    )
    pair_2 = turn_chips(pairs[2], 2)
    third, near2, far2, pair_3, pairs, singles, long_filter = order(
        (third, near2, far2, pair_3, pairs, singles, long_filter)
    )

    third = jnp.where(inner, farther, third)
    near3, far3 = spread(
        [far2[length : length + half], third], [near2[length + half :], third]
    )
    pair_1 = turn_chips(pairs[1], 1)
    single_3 = turn_chips(singles[3], 3)
    near3, far3, singles, long_filter, early = order((near3, far3, singles, long_filter, early))

    near4, far4 = spread([far3[half:length]], [near3[length:]])
    single_1, single_2 = turn_chips(singles[1], 1), turn_chips(singles[2], 2)
    pairs = [pairs[0], pair_1, pair_2, pair_3]
    singles = [singles[0], single_1, single_2, single_3]
    slots = (
        [block, pair, second, third],
        [near0, near1, near2, near3, near4],
        [far0, far1, far2, far3, far4],
    )
    return slots, pairs, singles, long_filter, early


def gather_plain(block, pairs, singles, long_filter, early):
    chips = lax.axis_size("chan") // 2
    slots = [turn_chips(block, s) if s else block for s in range(chips)]
    pairs, singles = (
        [turn_chips(x, s) if s else x for s, x in enumerate(w)] for w in (pairs, singles)
    )
    return slots, pairs, singles, long_filter, early


def project_kernel(plan, which, first, arrays, adds, at_ref, *refs):
    weights_refs, refs = refs[: len(which)], refs[len(which) :]
    pieces, refs = refs[:arrays], refs[arrays:]
    sums, refs = refs[: 2 * adds], refs[2 * adds :]
    own_ref, other_ref, weights, turned, values, weight_sems, sems = refs
    slots = len(plan)
    rows = own_ref.shape[0]
    length = own_ref.shape[1]
    step = pl.program_id(0)
    weight_copies = [
        pltpu.make_async_copy(weights_refs[s], weights.at[s], weight_sems.at[s])
        for s in range(len(which))
    ]
    copies = [
        [
            pltpu.make_async_copy(
                pieces[array].at[pl.ds(start, count)],
                values.at[s, pl.ds(target, count)],
                sems.at[5 * s + n],
            )
            for s in range(slots)
            for n, (array, start, count, target) in enumerate(plan[s])
            if target // length == q
        ]
        for q in range(4)
    ]

    @pl.when(step == 0)
    def _():
        for copy in weight_copies + copies[0] + copies[1]:
            copy.start()
        for copy in weight_copies:
            copy.wait()
        for s in range(slots):
            turned[s] = weights[at_ref[4 + s] - first].T

    for q in range(4):

        @pl.when(step == q)
        def _():
            for copy in copies[q]:
                copy.wait()
            if 0 < q < 3:
                for copy in copies[q + 1]:
                    copy.start()
            total = None
            for s in range(slots):
                part = lax.dot_general(
                    turned[s],
                    values[s, q * length : (q + 1) * length],
                    (((1,), (1,)), ((), ())),
                    preferred_element_type=F32,
                )
                total = part if total is None else total + part
            own, other = total[:rows], total[rows:]
            if adds:
                own, other = own + sums[0][...], other + sums[1][...]
            own_ref[...] = own
            other_ref[...] = other.astype(other_ref.dtype)


def project_plain(slots, weights):
    total = 0.0
    for block, piece in zip(slots, weights):
        full = lax.all_gather(block, "ctx", axis=0, tiled=True)
        total = total + jnp.einsum("td,dc->ct", full, piece, preferred_element_type=F32)
    rows = total.shape[0] // 2
    return total[:rows], total[rows:]


def project(slots, weights, first, last, sums=(), send=BF16):
    blocks, near, far = slots
    length, depth = blocks[0].shape
    half = length // 2
    rows = weights[0].shape[1] // 2
    me = lax.axis_index("ctx")
    place = lax.axis_index("chan") // 2
    swapped = jnp.where((place == 1) | (place == 2), 1, 0)
    at = jnp.stack(
        [me ^ q for q in range(4)] + [0 * me, 0 * me + 1, 2 + swapped, 3 - swapped][first:last]
    )
    arrays, plan = [], []

    def place_of(x):
        for n, y in enumerate(arrays):
            if y is x:
                return n
        arrays.append(x)
        return len(arrays) - 1

    for s in range(first, last):
        skip = (0, 0, length, half)[s]
        corner, row = ((2, 0), (2, half), (3, 0), (4, 0))[s]
        plan.append(
            (
                (place_of(blocks[s]), 0, length, 0),
                (place_of(near[s]), skip, length, length),
                (place_of(far[s]), skip, length, 2 * length),
                (place_of(near[corner]), row, half, 3 * length),
                (place_of(far[corner]), row, half, 3 * length + half),
            )
        )
    spec = pl.BlockSpec((rows, length), lambda g, at: (0, at[g]))
    return pl.pallas_call(
        functools.partial(project_kernel, plan, range(len(weights)), first, len(arrays), len(sums) // 2),
        grid_spec=pltpu.PrefetchScalarGridSpec(
            num_scalar_prefetch=1,
            grid=(4,),
            in_specs=[pl.BlockSpec(memory_space=pl.ANY)] * (len(weights) + len(arrays)) + [spec] * len(sums),
            out_specs=[spec] * 2,
            scratch_shapes=[
                pltpu.VMEM((len(weights), *weights[0].shape), BF16),
                pltpu.VMEM((last - first, 2 * rows, depth), BF16),
                pltpu.VMEM((last - first, 4 * length, depth), BF16),
                pltpu.SemaphoreType.DMA((len(weights),)),
                pltpu.SemaphoreType.DMA((5 * (last - first),)),
            ],
        ),
        out_shape=[
            jax.ShapeDtypeStruct((rows, 4 * length), F32),
            jax.ShapeDtypeStruct((rows, 4 * length), send),
        ],
        compiler_params=pltpu.CompilerParams(vmem_limit_bytes=PROJECT_LIMIT),
        name="project",
    )(at.astype(jnp.int32), *weights, *arrays, *sums)


def body(tokens, in_proj, short_taps, long_filter, skip_gain):
    length, depth = tokens.shape
    cycle = lax.axis_size("ctx")
    size = lax.axis_size("chan")
    chips = size // 2
    me = lax.axis_index("ctx")
    place = lax.axis_index("chan") // 2
    core = lax.axis_index("chan") % 2
    few = in_proj.shape[2] // (size * cycle)
    span = length * cycle
    high, low = (jnp.asarray(t) for t in wave_tables(length))
    pairs, singles = pick_columns(in_proj, chips, few, place, core, me, cycle)
    fits = cycle == 4 and chips == 4 and length % 512 == 0 and depth % 128 == 0
    own_taps = lax.dynamic_slice_in_dim(short_taps, me * few, few, axis=1)
    own_skip = lax.dynamic_slice_in_dim(skip_gain, me * few, few)[:, None]
    slots, pairs, singles, long_filter, (own_taps, own_skip) = (gather if fits else gather_plain)(
        tokens, pairs, singles, long_filter, (own_taps, own_skip)
    )
    moved_filter = lax.all_to_all(
        long_filter.reshape(cycle, few, length), "ctx", split_axis=0, concat_axis=0, tiled=True
    )
    if fits:
        mine, send = project(slots, pairs, 0, 4)
        send, singles, moved_filter = lax.optimization_barrier((send, singles, moved_filter))
    else:
        mine, send = project_plain(slots, pairs)
    waves = filter_waves(moved_filter, high, low)
    theirs = swap(send, "chan", 1)
    answer = convolve(
        mine.reshape(2, few, span), theirs.reshape(2, few, span), own_taps, own_skip, waves, high, low
    )
    mine, send = project(slots, singles, 0, 4) if fits else project_plain(slots, singles)
    gated = gate(mine, swap(send, "chan", 1), own_taps, answer, cycle)
    moved = lax.all_to_all(gated, "ctx", split_axis=0, concat_axis=0, tiled=True)
    return moved.reshape(cycle * few, length)


def solution(mesh):
    in_specs = (
        P("ctx", "chan"),
        P(None, "chan", None),
        P(None, "chan", None),
        P("chan", "ctx"),
        P("chan"),
    )
    out_specs = P("chan", "ctx")
    return jax.shard_map(body, mesh=mesh, in_specs=in_specs, out_specs=out_specs, check_vma=False)
```

```python
import functools

import jax
import jax.numpy as jnp
import ml_dtypes
import numpy as np
from jax import lax
from jax.experimental import pallas as pl
from jax.experimental.pallas import tpu as pltpu
from jax.sharding import PartitionSpec as P

VMEM_LIMIT = 32 * 1024 * 1024
PROJECT_LIMIT = 60 * 1024 * 1024
F32 = jnp.float32
BF16 = jnp.bfloat16


def wave_tables(length):
    position = np.arange(length, dtype=np.int64)
    phase = (position[:, None] * (2 * position[None, :] + 1)) % (4 * length)
    angle = phase.astype(np.float64) * (2.0 * np.pi / (4 * length))
    table = np.concatenate([np.cos(angle), -np.sin(angle)], axis=1)
    high = table.astype(ml_dtypes.bfloat16)
    low = (table - high.astype(np.float64)).astype(ml_dtypes.bfloat16)
    return high, low


def spectrum(values, high, low):
    return jnp.dot(values, high, preferred_element_type=F32) + jnp.dot(
        values, low, preferred_element_type=F32
    )


def filter_waves(taps_ref, high, low):
    blocks, rows, length = taps_ref.shape
    waves = spectrum(taps_ref[...].reshape(blocks * rows, length), high, low) * (1.0 / length)
    lane = lax.broadcasted_iota(jnp.int32, (rows, length), 1)
    sign = jnp.where(lane % 2 == 0, 1.0, -1.0)
    out = []
    for m in range(blocks):
        real = waves[m * rows : (m + 1) * rows, :length]
        imag = waves[m * rows : (m + 1) * rows, length:]
        if m:
            real = real - sign * waves[(m - 1) * rows : m * rows, length:]
            imag = imag + sign * waves[(m - 1) * rows : m * rows, :length]
        out.append((real, imag))
    return out


def feature(own, other, params, stream):
    mixed = (own + other.astype(F32)).astype(BF16).astype(F32)
    lane = lax.broadcasted_iota(jnp.int32, mixed.shape, 1)
    one = jnp.where(lane >= 1, pltpu.roll(mixed, 1, 1), 0.0)
    two = jnp.where(lane >= 2, pltpu.roll(mixed, 2, 1), 0.0)
    taps = [params[:, 3 * stream + n : 3 * stream + n + 1] for n in range(3)]
    return taps[0] * mixed + taps[1] * one + taps[2] * two


def conv_kernel(own_ref, other_ref, params_ref, filter_ref, high_ref, low_ref, out_ref):
    blocks, rows, length = filter_ref.shape
    params = params_ref[...]
    product = (
        feature(own_ref[0], other_ref[0], params, 1) * feature(own_ref[1], other_ref[1], params, 2)
    ).astype(BF16)
    values = jnp.concatenate(
        [product[:, p * length : (p + 1) * length] for p in range(blocks)], axis=0
    )
    high = high_ref[...]
    low = low_ref[...]
    waves = spectrum(values, high, low)
    taps = filter_waves(filter_ref, high, low)
    pieces = []
    for p in range(blocks):
        real = jnp.zeros((rows, length), F32)
        imag = jnp.zeros((rows, length), F32)
        for q in range(p + 1):
            in_real = waves[q * rows : (q + 1) * rows, :length]
            in_imag = waves[q * rows : (q + 1) * rows, length:]
            tap_real, tap_imag = taps[p - q]
            real = real + (in_real * tap_real - in_imag * tap_imag)
            imag = imag + (in_real * tap_imag + in_imag * tap_real)
        pieces.append(jnp.concatenate([real, imag], axis=1))
    total = jnp.concatenate(pieces, axis=0)
    total_high = total.astype(BF16)
    total_low = (total - total_high.astype(F32)).astype(BF16)
    dims = (((1,), (1,)), ((), ()))
    back = (
        lax.dot_general(total_high, high, dims, preferred_element_type=F32)
        + lax.dot_general(total_low, high, dims, preferred_element_type=F32)
        + lax.dot_general(total_high, low, dims, preferred_element_type=F32)
    )
    skip = params[:, 9:10]
    for p in range(blocks):
        span = slice(p * length, (p + 1) * length)
        out_ref[:, span] = back[p * rows : (p + 1) * rows] + skip * product[:, span].astype(F32)


def convolve(own, other, params, moved_filter, high, low):
    streams, rows, span = own.shape
    blocks, _, length = moved_filter.shape
    step = min(rows, 64)
    return pl.pallas_call(
        conv_kernel,
        grid=(rows // step,),
        in_specs=[
            pl.BlockSpec((streams, step, span), lambda g: (0, g, 0)),
            pl.BlockSpec((streams, step, span), lambda g: (0, g, 0)),
            pl.BlockSpec((step, 10), lambda g: (g, 0)),
            pl.BlockSpec((blocks, step, length), lambda g: (0, g, 0)),
            pl.BlockSpec((length, 2 * length), lambda g: (0, 0)),
            pl.BlockSpec((length, 2 * length), lambda g: (0, 0)),
        ],
        out_specs=pl.BlockSpec((step, span), lambda g: (g, 0)),
        out_shape=jax.ShapeDtypeStruct((rows, span), F32),
        compiler_params=pltpu.CompilerParams(vmem_limit_bytes=PROJECT_LIMIT),
        name="convolve",
    )(own, other, params, moved_filter, high, low)


def gate_kernel(own_ref, other_ref, params_ref, answer_ref, out_ref):
    blocks, _, length = out_ref.shape
    gated = (feature(own_ref[...], other_ref[...], params_ref[...], 0) * answer_ref[...]).astype(BF16)
    for p in range(blocks):
        out_ref[p] = gated[:, p * length : (p + 1) * length]


def gate(own, other, params, answer, blocks):
    rows, span = own.shape
    step = min(rows, 64)
    return pl.pallas_call(
        gate_kernel,
        grid=(rows // step,),
        in_specs=[
            pl.BlockSpec((step, span), lambda g: (g, 0)),
            pl.BlockSpec((step, span), lambda g: (g, 0)),
            pl.BlockSpec((step, 10), lambda g: (g, 0)),
            pl.BlockSpec((step, span), lambda g: (g, 0)),
        ],
        out_specs=pl.BlockSpec((blocks, step, span // blocks), lambda g: (0, g, 0)),
        out_shape=jax.ShapeDtypeStruct((blocks, rows, span // blocks), BF16),
        compiler_params=pltpu.CompilerParams(vmem_limit_bytes=VMEM_LIMIT),
        name="gate",
    )(own, other, params, answer)


def swap(x, axis, bit):
    return lax.ppermute(x, axis, [(i, i ^ bit) for i in range(lax.axis_size(axis))])


def pick_kernel(at_ref, in_proj_ref, *refs):
    chips = len(refs) // 2
    few = in_proj_ref.shape[2]
    for s in range(chips):

        @pl.when(pl.program_id(0) // 2 == s)
        def _():
            refs[s][:, :few] = in_proj_ref[1]
            refs[s][:, few:] = in_proj_ref[2]
            refs[chips + s][...] = in_proj_ref[0]


def pick_columns(in_proj, chips, few, place, core, me, cycle):
    depth = in_proj.shape[1]
    order = [2 * (place ^ s) + (core ^ side) for s in range(chips) for side in range(2)]
    at = jnp.stack([o * cycle + me for o in order]).astype(jnp.int32)
    if few % 128:
        parts = [
            [lax.dynamic_slice_in_dim(in_proj[k], at[n] * few, few, axis=1) for n in range(2 * chips)]
            for k in range(3)
        ]
        pairs = [
            jnp.concatenate([parts[k][2 * s + side] for side in range(2) for k in (1, 2)], axis=1)
            for s in range(chips)
        ]
        singles = [jnp.concatenate(parts[0][2 * s : 2 * s + 2], axis=1) for s in range(chips)]
        return pairs, singles

    def target(s):
        return lambda g, at: (0, jnp.clip(g - 2 * s, 0, 1))

    outs = pl.pallas_call(
        pick_kernel,
        grid_spec=pltpu.PrefetchScalarGridSpec(
            num_scalar_prefetch=1,
            grid=(2 * chips,),
            in_specs=[pl.BlockSpec((3, depth, few), lambda g, at: (0, 0, at[g]))],
            out_specs=[pl.BlockSpec((depth, 2 * few), target(s)) for s in range(chips)]
            + [pl.BlockSpec((depth, few), target(s)) for s in range(chips)],
        ),
        out_shape=[jax.ShapeDtypeStruct((depth, 4 * few), BF16)] * chips
        + [jax.ShapeDtypeStruct((depth, 2 * few), BF16)] * chips,
        compiler_params=pltpu.CompilerParams(vmem_limit_bytes=PROJECT_LIMIT),
        name="pick_columns",
    )(at, in_proj)
    return outs[:chips], outs[chips:]


def swap_far(block):
    return swap(block, "ctx", 1), swap(block, "ctx", 2)


def move_chips(x, pairs):
    return lax.ppermute(x, "chan", [(2 * a + k, 2 * b + k) for a, b in pairs for k in range(2)])


def turn_chips(x, s):
    return move_chips(x, [(z, z ^ s) for z in range(lax.axis_size("chan") // 2)])


def gather(block, pairs, singles, long_filter, early):
    place = lax.axis_index("chan") // 2
    middle = [(1, 2), (2, 1)]
    ends = [(1, 0), (2, 3)]
    inner = (place == 1) | (place == 2)
    order = lax.optimization_barrier
    pairs, singles = list(pairs), list(singles)
    length = block.shape[0]
    half = length // 2

    def spread(to_near, to_far):
        return swap(jnp.concatenate(to_near), "ctx", 1), swap(jnp.concatenate(to_far), "ctx", 2)

    pair = move_chips(block, [(0, 1), (1, 0), (2, 3), (3, 2)])
    across = move_chips(block, middle)
    near0, far0 = swap_far(block)
    pair, across, near0, far0, pairs, singles, long_filter = order(
        (pair, across, near0, far0, pairs, singles, long_filter)
    )

    farther = move_chips(pair, middle)
    second = move_chips(across, ends)
    near1, far1 = swap_far(pair)
    pairs[3] = turn_chips(pairs[3], 3)
    pair_3 = pairs.pop()
    farther, second, near1, far1, pairs, singles, long_filter = order(
        (farther, second, near1, far1, pairs, singles, long_filter)
    )

    second = jnp.where(inner, across, second)
    third = move_chips(farther, ends)
    near2, far2 = spread(
        [far0[:half], far1[:half], second], [near0[half:], near1[half:], second]
    )
    pair_2 = turn_chips(pairs[2], 2)
    third, near2, far2, pair_3, pairs, singles, long_filter = order(
        (third, near2, far2, pair_3, pairs, singles, long_filter)
    )

    third = jnp.where(inner, farther, third)
    near3, far3 = spread(
        [far2[length : length + half], third], [near2[length + half :], third]
    )
    pair_1 = turn_chips(pairs[1], 1)
    single_3 = turn_chips(singles[3], 3)
    near3, far3, singles, long_filter, early = order((near3, far3, singles, long_filter, early))

    near4, far4 = spread([far3[half:length]], [near3[length:]])
    single_1, single_2 = turn_chips(singles[1], 1), turn_chips(singles[2], 2)
    pairs = [pairs[0], pair_1, pair_2, pair_3]
    singles = [singles[0], single_1, single_2, single_3]
    slots = (
        [block, pair, second, third],
        [near0, near1, near2, near3, near4],
        [far0, far1, far2, far3, far4],
    )
    return slots, pairs, singles, long_filter, early


def gather_plain(block, pairs, singles, long_filter, early):
    chips = lax.axis_size("chan") // 2
    slots = [turn_chips(block, s) if s else block for s in range(chips)]
    pairs, singles = (
        [turn_chips(x, s) if s else x for s, x in enumerate(w)] for w in (pairs, singles)
    )
    return slots, pairs, singles, long_filter, early


def project_kernel(plan, which, first, arrays, adds, at_ref, *refs):
    weights_refs, refs = refs[: len(which)], refs[len(which) :]
    pieces, refs = refs[:arrays], refs[arrays:]
    sums, refs = refs[: 2 * adds], refs[2 * adds :]
    own_ref, other_ref, weights, turned, values, weight_sems, sems = refs
    slots = len(plan)
    rows = own_ref.shape[0]
    length = own_ref.shape[1]
    step = pl.program_id(0)
    weight_copies = [
        pltpu.make_async_copy(weights_refs[s], weights.at[s], weight_sems.at[s])
        for s in range(len(which))
    ]
    copies = [
        [
            pltpu.make_async_copy(
                pieces[array].at[pl.ds(start, count)],
                values.at[s, pl.ds(target, count)],
                sems.at[5 * s + n],
            )
            for s in range(slots)
            for n, (array, start, count, target) in enumerate(plan[s])
            if target // length == q
        ]
        for q in range(4)
    ]

    @pl.when(step == 0)
    def _():
        for copy in weight_copies + copies[0] + copies[1]:
            copy.start()
        for copy in weight_copies:
            copy.wait()
        for s in range(slots):
            turned[s] = weights[at_ref[4 + s] - first].T

    for q in range(4):

        @pl.when(step == q)
        def _():
            for copy in copies[q]:
                copy.wait()
            if 0 < q < 3:
                for copy in copies[q + 1]:
                    copy.start()
            total = None
            for s in range(slots):
                part = lax.dot_general(
                    turned[s],
                    values[s, q * length : (q + 1) * length],
                    (((1,), (1,)), ((), ())),
                    preferred_element_type=F32,
                )
                total = part if total is None else total + part
            own, other = total[:rows], total[rows:]
            if adds:
                own, other = own + sums[0][...], other + sums[1][...]
            own_ref[...] = own
            other_ref[...] = other.astype(other_ref.dtype)


def project_plain(slots, weights):
    total = 0.0
    for block, piece in zip(slots, weights):
        full = lax.all_gather(block, "ctx", axis=0, tiled=True)
        total = total + jnp.einsum("td,dc->ct", full, piece, preferred_element_type=F32)
    rows = total.shape[0] // 2
    return total[:rows], total[rows:]


def project(at, slots, weights, first, last, sums=(), send=F32):
    blocks, near, far = slots
    length, depth = blocks[0].shape
    half = length // 2
    rows = weights[0].shape[1] // 2
    arrays, plan = [], []

    def place_of(x):
        for n, y in enumerate(arrays):
            if y is x:
                return n
        arrays.append(x)
        return len(arrays) - 1

    for s in range(first, last):
        skip = (0, 0, length, half)[s]
        corner, row = ((2, 0), (2, half), (3, 0), (4, 0))[s]
        plan.append(
            (
                (place_of(blocks[s]), 0, length, 0),
                (place_of(near[s]), skip, length, length),
                (place_of(far[s]), skip, length, 2 * length),
                (place_of(near[corner]), row, half, 3 * length),
                (place_of(far[corner]), row, half, 3 * length + half),
            )
        )
    spec = pl.BlockSpec((rows, length), lambda g, at: (0, at[g]))
    return pl.pallas_call(
        functools.partial(project_kernel, plan, range(len(weights)), first, len(arrays), len(sums) // 2),
        grid_spec=pltpu.PrefetchScalarGridSpec(
            num_scalar_prefetch=1,
            grid=(4,),
            in_specs=[pl.BlockSpec(memory_space=pl.ANY)] * (len(weights) + len(arrays)) + [spec] * len(sums),
            out_specs=[spec] * 2,
            scratch_shapes=[
                pltpu.VMEM((len(weights), *weights[0].shape), BF16),
                pltpu.VMEM((last - first, 2 * rows, depth), BF16),
                pltpu.VMEM((last - first, 4 * length, depth), BF16),
                pltpu.SemaphoreType.DMA((len(weights),)),
                pltpu.SemaphoreType.DMA((5 * (last - first),)),
            ],
        ),
        out_shape=[
            jax.ShapeDtypeStruct((rows, 4 * length), F32),
            jax.ShapeDtypeStruct((rows, 4 * length), send),
        ],
        compiler_params=pltpu.CompilerParams(vmem_limit_bytes=PROJECT_LIMIT),
        name="project",
    )(at, *weights, *arrays, *sums)


def body(tokens, in_proj, short_taps, long_filter, skip_gain):
    length, depth = tokens.shape
    cycle = lax.axis_size("ctx")
    size = lax.axis_size("chan")
    chips = size // 2
    me = lax.axis_index("ctx")
    place = lax.axis_index("chan") // 2
    core = lax.axis_index("chan") % 2
    few = in_proj.shape[2] // (size * cycle)
    span = length * cycle
    high, low = (jnp.asarray(t) for t in wave_tables(length))
    pairs, singles = pick_columns(in_proj, chips, few, place, core, me, cycle)
    fits = cycle == 4 and chips == 4 and length % 512 == 0 and depth % 128 == 0
    own_taps = lax.dynamic_slice_in_dim(short_taps, me * few, few, axis=1)
    own_skip = lax.dynamic_slice_in_dim(skip_gain, me * few, few)[:, None]
    params = jnp.concatenate([own_taps[0], own_taps[1], own_taps[2], own_skip], axis=1)
    swapped = jnp.where((place == 1) | (place == 2), 1, 0)
    at = jnp.stack([me ^ q for q in range(4)] + [0 * me, 0 * me + 1, 2 + swapped, 3 - swapped])
    slots, pairs, singles, long_filter, (params, at) = (gather if fits else gather_plain)(
        tokens, pairs, singles, long_filter, (params, at.astype(jnp.int32))
    )
    moved_filter = lax.all_to_all(
        long_filter.reshape(cycle, few, length), "ctx", split_axis=0, concat_axis=0, tiled=True
    )
    if fits:
        mine, send = project(at, slots, pairs, 0, 4)
        send, singles, moved_filter = lax.optimization_barrier((send, singles, moved_filter))
    else:
        mine, send = project_plain(slots, pairs)
    theirs = swap(send, "chan", 1)
    answer = convolve(
        mine.reshape(2, few, span), theirs.reshape(2, few, span), params, moved_filter, high, low
    )
    mine, send = project(at, slots, singles, 0, 4) if fits else project_plain(slots, singles)
    gated = gate(mine, swap(send, "chan", 1), params, answer, cycle)
    moved = lax.all_to_all(gated, "ctx", split_axis=0, concat_axis=0, tiled=True)
    return moved.reshape(cycle * few, length)


def solution(mesh):
    in_specs = (
        P("ctx", "chan"),
        P(None, "chan", None),
        P(None, "chan", None),
        P("chan", "ctx"),
        P("chan"),
    )
    out_specs = P("chan", "ctx")
    return jax.shard_map(body, mesh=mesh, in_specs=in_specs, out_specs=out_specs, check_vma=False)
```

```python
import functools

import jax
import jax.numpy as jnp
import ml_dtypes
import numpy as np
from jax import lax
from jax.experimental import pallas as pl
from jax.experimental.pallas import tpu as pltpu
from jax.sharding import PartitionSpec as P

VMEM_LIMIT = 32 * 1024 * 1024
PROJECT_LIMIT = 52 * 1024 * 1024
CONVOLVE_LIMIT = 60 * 1024 * 1024
F32 = jnp.float32
BF16 = jnp.bfloat16


def wave_tables(length):
    position = np.arange(length, dtype=np.int64)
    phase = (position[:, None] * (2 * position[None, :] + 1)) % (4 * length)
    angle = phase.astype(np.float64) * (2.0 * np.pi / (4 * length))
    table = np.concatenate([np.cos(angle), -np.sin(angle)], axis=1)
    high = table.astype(ml_dtypes.bfloat16)
    low = (table - high.astype(np.float64)).astype(ml_dtypes.bfloat16)
    return high, low


def spectrum(values, high, low):
    return jnp.dot(values, high, preferred_element_type=F32) + jnp.dot(
        values, low, preferred_element_type=F32
    )


def filter_waves(taps_ref, high, low):
    blocks, rows, length = taps_ref.shape
    waves = spectrum(taps_ref[...].reshape(blocks * rows, length), high, low) * (1.0 / length)
    lane = lax.broadcasted_iota(jnp.int32, (rows, length), 1)
    sign = jnp.where(lane % 2 == 0, 1.0, -1.0)
    out = []
    for m in range(blocks):
        real = waves[m * rows : (m + 1) * rows, :length]
        imag = waves[m * rows : (m + 1) * rows, length:]
        if m:
            real = real - sign * waves[(m - 1) * rows : m * rows, length:]
            imag = imag + sign * waves[(m - 1) * rows : m * rows, :length]
        out.append((real, imag))
    return out


def feature(own, other, params, stream):
    mixed = (own + other.astype(F32)).astype(BF16).astype(F32)
    lane = lax.broadcasted_iota(jnp.int32, mixed.shape, 1)
    one = jnp.where(lane >= 1, pltpu.roll(mixed, 1, 1), 0.0)
    two = jnp.where(lane >= 2, pltpu.roll(mixed, 2, 1), 0.0)
    taps = [params[:, 3 * stream + n : 3 * stream + n + 1] for n in range(3)]
    return taps[0] * mixed + taps[1] * one + taps[2] * two


def conv_kernel(own_ref, other_ref, params_ref, filter_ref, high_ref, low_ref, out_ref):
    blocks, rows, length = filter_ref.shape
    params = params_ref[...]
    product = (
        feature(own_ref[0], other_ref[0], params, 1) * feature(own_ref[1], other_ref[1], params, 2)
    ).astype(BF16)
    values = jnp.concatenate(
        [product[:, p * length : (p + 1) * length] for p in range(blocks)], axis=0
    )
    high = high_ref[...]
    low = low_ref[...]
    waves = spectrum(values, high, low)
    taps = filter_waves(filter_ref, high, low)
    pieces = []
    for p in range(blocks):
        real = jnp.zeros((rows, length), F32)
        imag = jnp.zeros((rows, length), F32)
        for q in range(p + 1):
            in_real = waves[q * rows : (q + 1) * rows, :length]
            in_imag = waves[q * rows : (q + 1) * rows, length:]
            tap_real, tap_imag = taps[p - q]
            real = real + (in_real * tap_real - in_imag * tap_imag)
            imag = imag + (in_real * tap_imag + in_imag * tap_real)
        pieces.append(jnp.concatenate([real, imag], axis=1))
    total = jnp.concatenate(pieces, axis=0)
    total_high = total.astype(BF16)
    total_low = (total - total_high.astype(F32)).astype(BF16)
    dims = (((1,), (1,)), ((), ()))
    back = (
        lax.dot_general(total_high, high, dims, preferred_element_type=F32)
        + lax.dot_general(total_low, high, dims, preferred_element_type=F32)
        + lax.dot_general(total_high, low, dims, preferred_element_type=F32)
    )
    skip = params[:, 9:10]
    for p in range(blocks):
        span = slice(p * length, (p + 1) * length)
        out_ref[:, span] = back[p * rows : (p + 1) * rows] + skip * product[:, span].astype(F32)


def convolve(own, other, params, moved_filter, high, low):
    streams, rows, span = own.shape
    blocks, _, length = moved_filter.shape
    step = min(rows, 64)
    return pl.pallas_call(
        conv_kernel,
        grid=(rows // step,),
        in_specs=[
            pl.BlockSpec((streams, step, span), lambda g: (0, g, 0)),
            pl.BlockSpec((streams, step, span), lambda g: (0, g, 0)),
            pl.BlockSpec((step, 10), lambda g: (g, 0)),
            pl.BlockSpec((blocks, step, length), lambda g: (0, g, 0)),
            pl.BlockSpec((length, 2 * length), lambda g: (0, 0)),
            pl.BlockSpec((length, 2 * length), lambda g: (0, 0)),
        ],
        out_specs=pl.BlockSpec((step, span), lambda g: (g, 0)),
        out_shape=jax.ShapeDtypeStruct((rows, span), F32),
        compiler_params=pltpu.CompilerParams(vmem_limit_bytes=CONVOLVE_LIMIT),
        name="convolve",
    )(own, other, params, moved_filter, high, low)


def gate_kernel(own_ref, other_ref, params_ref, answer_ref, out_ref):
    blocks, _, length = out_ref.shape
    gated = (feature(own_ref[...], other_ref[...], params_ref[...], 0) * answer_ref[...]).astype(BF16)
    for p in range(blocks):
        out_ref[p] = gated[:, p * length : (p + 1) * length]


def gate(own, other, params, answer, blocks):
    rows, span = own.shape
    step = min(rows, 64)
    return pl.pallas_call(
        gate_kernel,
        grid=(rows // step,),
        in_specs=[
            pl.BlockSpec((step, span), lambda g: (g, 0)),
            pl.BlockSpec((step, span), lambda g: (g, 0)),
            pl.BlockSpec((step, 10), lambda g: (g, 0)),
            pl.BlockSpec((step, span), lambda g: (g, 0)),
        ],
        out_specs=pl.BlockSpec((blocks, step, span // blocks), lambda g: (0, g, 0)),
        out_shape=jax.ShapeDtypeStruct((blocks, rows, span // blocks), BF16),
        compiler_params=pltpu.CompilerParams(vmem_limit_bytes=VMEM_LIMIT),
        name="gate",
    )(own, other, params, answer)


def swap(x, axis, bit):
    return lax.ppermute(x, axis, [(i, i ^ bit) for i in range(lax.axis_size(axis))])


def pick_kernel(at_ref, in_proj_ref, *refs):
    chips = len(refs) // 2
    few = in_proj_ref.shape[2]
    for s in range(chips):

        @pl.when(pl.program_id(0) // 2 == s)
        def _():
            refs[s][:, :few] = in_proj_ref[1]
            refs[s][:, few:] = in_proj_ref[2]
            refs[chips + s][...] = in_proj_ref[0]


def pick_columns(in_proj, chips, few, place, core, me, cycle):
    depth = in_proj.shape[1]
    order = [2 * (place ^ s) + (core ^ side) for s in range(chips) for side in range(2)]
    at = jnp.stack([o * cycle + me for o in order]).astype(jnp.int32)
    if few % 128:
        parts = [
            [lax.dynamic_slice_in_dim(in_proj[k], at[n] * few, few, axis=1) for n in range(2 * chips)]
            for k in range(3)
        ]
        pairs = [
            jnp.concatenate([parts[k][2 * s + side] for side in range(2) for k in (1, 2)], axis=1)
            for s in range(chips)
        ]
        singles = [jnp.concatenate(parts[0][2 * s : 2 * s + 2], axis=1) for s in range(chips)]
        return pairs, singles

    def target(s):
        return lambda g, at: (0, jnp.clip(g - 2 * s, 0, 1))

    outs = pl.pallas_call(
        pick_kernel,
        grid_spec=pltpu.PrefetchScalarGridSpec(
            num_scalar_prefetch=1,
            grid=(2 * chips,),
            in_specs=[pl.BlockSpec((3, depth, few), lambda g, at: (0, 0, at[g]))],
            out_specs=[pl.BlockSpec((depth, 2 * few), target(s)) for s in range(chips)]
            + [pl.BlockSpec((depth, few), target(s)) for s in range(chips)],
        ),
        out_shape=[jax.ShapeDtypeStruct((depth, 4 * few), BF16)] * chips
        + [jax.ShapeDtypeStruct((depth, 2 * few), BF16)] * chips,
        compiler_params=pltpu.CompilerParams(vmem_limit_bytes=CONVOLVE_LIMIT),
        name="pick_columns",
    )(at, in_proj)
    return outs[:chips], outs[chips:]


def swap_far(block):
    return swap(block, "ctx", 1), swap(block, "ctx", 2)


def move_chips(x, pairs):
    return lax.ppermute(x, "chan", [(2 * a + k, 2 * b + k) for a, b in pairs for k in range(2)])


def turn_chips(x, s):
    return move_chips(x, [(z, z ^ s) for z in range(lax.axis_size("chan") // 2)])


def gather(block, pairs, singles, long_filter, early):
    place = lax.axis_index("chan") // 2
    middle = [(1, 2), (2, 1)]
    ends = [(1, 0), (2, 3)]
    inner = (place == 1) | (place == 2)
    order = lax.optimization_barrier
    pairs, singles = list(pairs), list(singles)
    length = block.shape[0]
    half = length // 2

    def spread(to_near, to_far):
        to_near, to_far = jnp.concatenate(to_near), jnp.concatenate(to_far)
        return to_near, swap(to_near, "ctx", 1), swap(to_far, "ctx", 2)

    pair = move_chips(block, [(0, 1), (1, 0), (2, 3), (3, 2)])
    across = move_chips(block, middle)
    near0, far0 = swap_far(block)
    pair, across, near0, far0, pairs, singles, long_filter = order(
        (pair, across, near0, far0, pairs, singles, long_filter)
    )

    farther = move_chips(pair, middle)
    second = move_chips(across, ends)
    near1, far1 = swap_far(pair)
    pairs[3] = turn_chips(pairs[3], 3)
    pair_3 = pairs.pop()
    farther, second, near1, far1, pairs, singles, long_filter = order(
        (farther, second, near1, far1, pairs, singles, long_filter)
    )

    second = jnp.where(inner, across, second)
    third = move_chips(farther, ends)
    second, near2, far2 = spread(
        [far0[:half], far1[:half], second], [near0[half:], near1[half:], second]
    )
    pair_2 = turn_chips(pairs[2], 2)
    third, near2, far2, pair_3, pairs, singles, long_filter = order(
        (third, near2, far2, pair_3, pairs, singles, long_filter)
    )

    third = jnp.where(inner, farther, third)
    third, near3, far3 = spread(
        [far2[length : length + half], third], [near2[length + half :], third]
    )
    pair_1 = turn_chips(pairs[1], 1)
    single_3 = turn_chips(singles[3], 3)
    near3, far3, singles, long_filter, early = order((near3, far3, singles, long_filter, early))

    _, near4, far4 = spread([far3[half:length]], [near3[length:]])
    single_1, single_2 = turn_chips(singles[1], 1), turn_chips(singles[2], 2)
    pairs = [pairs[0], pair_1, pair_2, pair_3]
    singles = [singles[0], single_1, single_2, single_3]
    slots = (
        [block, pair, second, third],
        [near0, near1, near2, near3, near4],
        [far0, far1, far2, far3, far4],
    )
    return slots, pairs, singles, long_filter, early


def gather_plain(block, pairs, singles, long_filter, early):
    chips = lax.axis_size("chan") // 2
    slots = [turn_chips(block, s) if s else block for s in range(chips)]
    pairs, singles = (
        [turn_chips(x, s) if s else x for s, x in enumerate(w)] for w in (pairs, singles)
    )
    return slots, pairs, singles, long_filter, early


def project_kernel(plan, which, first, arrays, adds, at_ref, *refs):
    weights_refs, refs = refs[: len(which)], refs[len(which) :]
    pieces, refs = refs[:arrays], refs[arrays:]
    sums, refs = refs[: 2 * adds], refs[2 * adds :]
    own_ref, other_ref, weights, turned, values, weight_sems, sems = refs
    slots = len(plan)
    rows = own_ref.shape[0]
    length = own_ref.shape[1]
    step = pl.program_id(0)
    weight_copies = [
        pltpu.make_async_copy(weights_refs[s], weights.at[s], weight_sems.at[s])
        for s in range(len(which))
    ]
    copies = [
        [
            pltpu.make_async_copy(
                pieces[array].at[pl.ds(start, count)],
                values.at[s, pl.ds(target, count)],
                sems.at[5 * s + n],
            )
            for s in range(slots)
            for n, (array, start, count, target) in enumerate(plan[s])
            if target // length == q
        ]
        for q in range(4)
    ]

    @pl.when(step == 0)
    def _():
        for copy in weight_copies + copies[0] + copies[1]:
            copy.start()
        for copy in weight_copies:
            copy.wait()
        for s in range(slots):
            turned[s] = weights[at_ref[4 + s] - first].T

    for q in range(4):

        @pl.when(step == q)
        def _():
            for copy in copies[q]:
                copy.wait()
            if 0 < q < 3:
                for copy in copies[q + 1]:
                    copy.start()
            total = None
            for s in range(slots):
                part = lax.dot_general(
                    turned[s],
                    values[s, q * length : (q + 1) * length],
                    (((1,), (1,)), ((), ())),
                    preferred_element_type=F32,
                )
                total = part if total is None else total + part
            own, other = total[:rows], total[rows:]
            if adds:
                own, other = own + sums[0][...], other + sums[1][...]
            own_ref[...] = own
            other_ref[...] = other.astype(other_ref.dtype)


def project_plain(slots, weights):
    total = 0.0
    for block, piece in zip(slots, weights):
        full = lax.all_gather(block, "ctx", axis=0, tiled=True)
        total = total + jnp.einsum("td,dc->ct", full, piece, preferred_element_type=F32)
    rows = total.shape[0] // 2
    return total[:rows], total[rows:]


def project(at, slots, weights, first, last, sums=(), send=F32):
    blocks, near, far = slots
    length, depth = blocks[0].shape
    half = length // 2
    rows = weights[0].shape[1] // 2
    arrays, plan = [], []

    def place_of(x):
        for n, y in enumerate(arrays):
            if y is x:
                return n
        arrays.append(x)
        return len(arrays) - 1

    for s in range(first, last):
        skip = (0, 0, length, half)[s]
        corner, row = ((2, 0), (2, half), (3, 0), (4, 0))[s]
        plan.append(
            (
                (place_of(blocks[s]), skip, length, 0),
                (place_of(near[s]), skip, length, length),
                (place_of(far[s]), skip, length, 2 * length),
                (place_of(near[corner]), row, half, 3 * length),
                (place_of(far[corner]), row, half, 3 * length + half),
            )
        )
    spec = pl.BlockSpec((rows, length), lambda g, at: (0, at[g]))
    return pl.pallas_call(
        functools.partial(project_kernel, plan, range(len(weights)), first, len(arrays), len(sums) // 2),
        grid_spec=pltpu.PrefetchScalarGridSpec(
            num_scalar_prefetch=1,
            grid=(4,),
            in_specs=[pl.BlockSpec(memory_space=pl.ANY)] * (len(weights) + len(arrays)) + [spec] * len(sums),
            out_specs=[spec] * 2,
            scratch_shapes=[
                pltpu.VMEM((len(weights), *weights[0].shape), BF16),
                pltpu.VMEM((last - first, 2 * rows, depth), BF16),
                pltpu.VMEM((last - first, 4 * length, depth), BF16),
                pltpu.SemaphoreType.DMA((len(weights),)),
                pltpu.SemaphoreType.DMA((5 * (last - first),)),
            ],
        ),
        out_shape=[
            jax.ShapeDtypeStruct((rows, 4 * length), F32),
            jax.ShapeDtypeStruct((rows, 4 * length), send),
        ],
        compiler_params=pltpu.CompilerParams(vmem_limit_bytes=PROJECT_LIMIT),
        name="project",
    )(at, *weights, *arrays, *sums)


def body(tokens, in_proj, short_taps, long_filter, skip_gain):
    length, depth = tokens.shape
    cycle = lax.axis_size("ctx")
    size = lax.axis_size("chan")
    chips = size // 2
    me = lax.axis_index("ctx")
    place = lax.axis_index("chan") // 2
    core = lax.axis_index("chan") % 2
    few = in_proj.shape[2] // (size * cycle)
    span = length * cycle
    high, low = (jnp.asarray(t) for t in wave_tables(length))
    pairs, singles = pick_columns(in_proj, chips, few, place, core, me, cycle)
    fits = cycle == 4 and chips == 4 and length % 512 == 0 and depth % 128 == 0
    own_taps = lax.dynamic_slice_in_dim(short_taps, me * few, few, axis=1)
    own_skip = lax.dynamic_slice_in_dim(skip_gain, me * few, few)[:, None]
    params = jnp.concatenate([own_taps[0], own_taps[1], own_taps[2], own_skip], axis=1)
    swapped = jnp.where((place == 1) | (place == 2), 1, 0)
    at = jnp.stack([me ^ q for q in range(4)] + [0 * me, 0 * me + 1, 2 + swapped, 3 - swapped])
    slots, pairs, singles, long_filter, (params, at) = (gather if fits else gather_plain)(
        tokens, pairs, singles, long_filter, (params, at.astype(jnp.int32))
    )
    moved_filter = lax.all_to_all(
        long_filter.reshape(cycle, few, length), "ctx", split_axis=0, concat_axis=0, tiled=True
    )
    if fits:
        slots, moved_filter = lax.optimization_barrier((slots, moved_filter))
        mine, send = project(at, slots, pairs, 0, 4)
        send, singles = lax.optimization_barrier((send, singles))
    else:
        mine, send = project_plain(slots, pairs)
    theirs = swap(send, "chan", 1)
    answer = convolve(
        mine.reshape(2, few, span), theirs.reshape(2, few, span), params, moved_filter, high, low
    )
    mine, send = project(at, slots, singles, 0, 4) if fits else project_plain(slots, singles)
    gated = gate(mine, swap(send, "chan", 1), params, answer, cycle)
    moved = lax.all_to_all(gated, "ctx", split_axis=0, concat_axis=0, tiled=True)
    return moved.reshape(cycle * few, length)


def solution(mesh):
    in_specs = (
        P("ctx", "chan"),
        P(None, "chan", None),
        P(None, "chan", None),
        P("chan", "ctx"),
        P("chan"),
    )
    out_specs = P("chan", "ctx")
    return jax.shard_map(body, mesh=mesh, in_specs=in_specs, out_specs=out_specs, check_vma=False)
```

```python
import functools

import jax
import jax.numpy as jnp
import ml_dtypes
import numpy as np
from jax import lax
from jax.experimental import pallas as pl
from jax.experimental.pallas import tpu as pltpu
from jax.sharding import PartitionSpec as P

VMEM_LIMIT = 32 * 1024 * 1024
PROJECT_LIMIT = 52 * 1024 * 1024
CONVOLVE_LIMIT = 60 * 1024 * 1024
F32 = jnp.float32
BF16 = jnp.bfloat16


def wave_tables(length):
    position = np.arange(length, dtype=np.int64)
    phase = (position[:, None] * (2 * position[None, :] + 1)) % (4 * length)
    angle = phase.astype(np.float64) * (2.0 * np.pi / (4 * length))
    table = np.concatenate([np.cos(angle), -np.sin(angle)], axis=1)
    high = table.astype(ml_dtypes.bfloat16)
    low = (table - high.astype(np.float64)).astype(ml_dtypes.bfloat16)
    return high, low


def spectrum(values, high, low):
    return jnp.dot(values, high, preferred_element_type=F32) + jnp.dot(
        values, low, preferred_element_type=F32
    )


def filter_waves(taps_ref, high, low):
    blocks, rows, length = taps_ref.shape
    waves = spectrum(taps_ref[...].reshape(blocks * rows, length), high, low) * (1.0 / length)
    lane = lax.broadcasted_iota(jnp.int32, (rows, length), 1)
    sign = jnp.where(lane % 2 == 0, 1.0, -1.0)
    out = []
    for m in range(blocks):
        real = waves[m * rows : (m + 1) * rows, :length]
        imag = waves[m * rows : (m + 1) * rows, length:]
        if m:
            real = real - sign * waves[(m - 1) * rows : m * rows, length:]
            imag = imag + sign * waves[(m - 1) * rows : m * rows, :length]
        out.append((real, imag))
    return out


def feature(own, other, params, stream):
    mixed = (own + other.astype(F32)).astype(BF16).astype(F32)
    lane = lax.broadcasted_iota(jnp.int32, mixed.shape, 1)
    one = jnp.where(lane >= 1, pltpu.roll(mixed, 1, 1), 0.0)
    two = jnp.where(lane >= 2, pltpu.roll(mixed, 2, 1), 0.0)
    taps = [params[:, 3 * stream + n : 3 * stream + n + 1] for n in range(3)]
    return taps[0] * mixed + taps[1] * one + taps[2] * two


def conv_kernel(own_ref, other_ref, params_ref, filter_ref, high_ref, low_ref, out_ref):
    blocks, rows, length = filter_ref.shape
    params = params_ref[...]
    product = (
        feature(own_ref[0], other_ref[0], params, 1) * feature(own_ref[1], other_ref[1], params, 2)
    ).astype(BF16)
    values = jnp.concatenate(
        [product[:, p * length : (p + 1) * length] for p in range(blocks)], axis=0
    )
    high = high_ref[...]
    low = low_ref[...]
    waves = spectrum(values, high, low)
    taps = filter_waves(filter_ref, high, low)
    pieces = []
    for p in range(blocks):
        real = jnp.zeros((rows, length), F32)
        imag = jnp.zeros((rows, length), F32)
        for q in range(p + 1):
            in_real = waves[q * rows : (q + 1) * rows, :length]
            in_imag = waves[q * rows : (q + 1) * rows, length:]
            tap_real, tap_imag = taps[p - q]
            real = real + (in_real * tap_real - in_imag * tap_imag)
            imag = imag + (in_real * tap_imag + in_imag * tap_real)
        pieces.append(jnp.concatenate([real, imag], axis=1))
    total = jnp.concatenate(pieces, axis=0)
    total_high = total.astype(BF16)
    total_low = (total - total_high.astype(F32)).astype(BF16)
    dims = (((1,), (1,)), ((), ()))
    back = (
        lax.dot_general(total_high, high, dims, preferred_element_type=F32)
        + lax.dot_general(total_low, high, dims, preferred_element_type=F32)
        + lax.dot_general(total_high, low, dims, preferred_element_type=F32)
    )
    skip = params[:, 9:10]
    for p in range(blocks):
        span = slice(p * length, (p + 1) * length)
        out_ref[:, span] = back[p * rows : (p + 1) * rows] + skip * product[:, span].astype(F32)


def convolve(own, other, params, moved_filter, high, low):
    streams, rows, span = own.shape
    blocks, _, length = moved_filter.shape
    step = min(rows, 64)
    return pl.pallas_call(
        conv_kernel,
        grid=(rows // step,),
        in_specs=[
            pl.BlockSpec((streams, step, span), lambda g: (0, g, 0)),
            pl.BlockSpec((streams, step, span), lambda g: (0, g, 0)),
            pl.BlockSpec((step, 10), lambda g: (g, 0)),
            pl.BlockSpec((blocks, step, length), lambda g: (0, g, 0)),
            pl.BlockSpec((length, 2 * length), lambda g: (0, 0)),
            pl.BlockSpec((length, 2 * length), lambda g: (0, 0)),
        ],
        out_specs=pl.BlockSpec((step, span), lambda g: (g, 0)),
        out_shape=jax.ShapeDtypeStruct((rows, span), F32),
        compiler_params=pltpu.CompilerParams(vmem_limit_bytes=CONVOLVE_LIMIT),
        name="convolve",
    )(own, other, params, moved_filter, high, low)


def gate_kernel(own_ref, other_ref, params_ref, answer_ref, out_ref):
    blocks, _, length = out_ref.shape
    gated = (feature(own_ref[...], other_ref[...], params_ref[...], 0) * answer_ref[...]).astype(BF16)
    for p in range(blocks):
        out_ref[p] = gated[:, p * length : (p + 1) * length]


def gate(own, other, params, answer, blocks):
    rows, span = own.shape
    step = min(rows, 64)
    return pl.pallas_call(
        gate_kernel,
        grid=(rows // step,),
        in_specs=[
            pl.BlockSpec((step, span), lambda g: (g, 0)),
            pl.BlockSpec((step, span), lambda g: (g, 0)),
            pl.BlockSpec((step, 10), lambda g: (g, 0)),
            pl.BlockSpec((step, span), lambda g: (g, 0)),
        ],
        out_specs=pl.BlockSpec((blocks, step, span // blocks), lambda g: (0, g, 0)),
        out_shape=jax.ShapeDtypeStruct((blocks, rows, span // blocks), BF16),
        compiler_params=pltpu.CompilerParams(vmem_limit_bytes=VMEM_LIMIT),
        name="gate",
    )(own, other, params, answer)


def swap(x, axis, bit):
    return lax.ppermute(x, axis, [(i, i ^ bit) for i in range(lax.axis_size(axis))])


def pick_kernel(at_ref, in_proj_ref, *refs):
    chips = len(refs) // 2
    few = in_proj_ref.shape[2]
    for s in range(chips):

        @pl.when(pl.program_id(0) // 2 == s)
        def _():
            refs[s][:, :few] = in_proj_ref[1]
            refs[s][:, few:] = in_proj_ref[2]
            refs[chips + s][...] = in_proj_ref[0]


def pick_columns(in_proj, chips, few, place, core, me, cycle):
    depth = in_proj.shape[1]
    order = [2 * (place ^ s) + (core ^ side) for s in range(chips) for side in range(2)]
    at = jnp.stack([o * cycle + me for o in order]).astype(jnp.int32)
    if few % 128:
        parts = [
            [lax.dynamic_slice_in_dim(in_proj[k], at[n] * few, few, axis=1) for n in range(2 * chips)]
            for k in range(3)
        ]
        pairs = [
            jnp.concatenate([parts[k][2 * s + side] for side in range(2) for k in (1, 2)], axis=1)
            for s in range(chips)
        ]
        singles = [jnp.concatenate(parts[0][2 * s : 2 * s + 2], axis=1) for s in range(chips)]
        return pairs, singles

    def target(s):
        return lambda g, at: (0, jnp.clip(g - 2 * s, 0, 1))

    outs = pl.pallas_call(
        pick_kernel,
        grid_spec=pltpu.PrefetchScalarGridSpec(
            num_scalar_prefetch=1,
            grid=(2 * chips,),
            in_specs=[pl.BlockSpec((3, depth, few), lambda g, at: (0, 0, at[g]))],
            out_specs=[pl.BlockSpec((depth, 2 * few), target(s)) for s in range(chips)]
            + [pl.BlockSpec((depth, few), target(s)) for s in range(chips)],
        ),
        out_shape=[jax.ShapeDtypeStruct((depth, 4 * few), BF16)] * chips
        + [jax.ShapeDtypeStruct((depth, 2 * few), BF16)] * chips,
        compiler_params=pltpu.CompilerParams(vmem_limit_bytes=CONVOLVE_LIMIT),
        name="pick_columns",
    )(at, in_proj)
    return outs[:chips], outs[chips:]


def swap_far(block):
    return swap(block, "ctx", 1), swap(block, "ctx", 2)


def move_chips(x, pairs):
    return lax.ppermute(x, "chan", [(2 * a + k, 2 * b + k) for a, b in pairs for k in range(2)])


def turn_chips(x, s):
    return move_chips(x, [(z, z ^ s) for z in range(lax.axis_size("chan") // 2)])


def gather(block, pairs, singles, long_filter, early):
    place = lax.axis_index("chan") // 2
    middle = [(1, 2), (2, 1)]
    ends = [(1, 0), (2, 3)]
    inner = (place == 1) | (place == 2)
    order = lax.optimization_barrier
    pairs, singles = list(pairs), list(singles)
    length = block.shape[0]
    half = length // 2

    def spread(to_near, to_far):
        to_near, to_far = jnp.concatenate(to_near), jnp.concatenate(to_far)
        return to_near, swap(to_near, "ctx", 1), swap(to_far, "ctx", 2)

    pair = move_chips(block, [(0, 1), (1, 0), (2, 3), (3, 2)])
    across = move_chips(block, middle)
    near0, far0 = swap_far(block)
    pair, across, near0, far0, pairs, singles, long_filter = order(
        (pair, across, near0, far0, pairs, singles, long_filter)
    )

    farther = move_chips(pair, middle)
    second = move_chips(across, ends)
    near1, far1 = swap_far(pair)
    pairs[3] = turn_chips(pairs[3], 3)
    pair_3 = pairs.pop()
    farther, second, near1, far1, pairs, singles, long_filter = order(
        (farther, second, near1, far1, pairs, singles, long_filter)
    )

    second = jnp.where(inner, across, second)
    third = move_chips(farther, ends)
    second, near2, far2 = spread(
        [far0[:half], far1[:half], second], [near0[half:], near1[half:], second]
    )
    pair_2 = turn_chips(pairs[2], 2)
    third, near2, far2, pair_3, pairs, singles, long_filter = order(
        (third, near2, far2, pair_3, pairs, singles, long_filter)
    )

    third = jnp.where(inner, farther, third)
    third, near3, far3 = spread(
        [far2[length : length + half], third], [near2[length + half :], third]
    )
    pair_1 = turn_chips(pairs[1], 1)
    single_3 = turn_chips(singles[3], 3)
    near3, far3, singles, long_filter, early = order((near3, far3, singles, long_filter, early))

    _, near4, far4 = spread([far3[half:length]], [near3[length:]])
    single_1, single_2 = turn_chips(singles[1], 1), turn_chips(singles[2], 2)
    pairs = [pairs[0], pair_1, pair_2, pair_3]
    singles = [singles[0], single_1, single_2, single_3]
    slots = (
        [block, pair, second, third],
        [near0, near1, near2, near3, near4],
        [far0, far1, far2, far3, far4],
    )
    return slots, pairs, singles, long_filter, early


def gather_plain(block, pairs, singles, long_filter, early):
    chips = lax.axis_size("chan") // 2
    slots = [turn_chips(block, s) if s else block for s in range(chips)]
    pairs, singles = (
        [turn_chips(x, s) if s else x for s, x in enumerate(w)] for w in (pairs, singles)
    )
    return slots, pairs, singles, long_filter, early


def project_kernel(plan, which, first, arrays, adds, at_ref, *refs):
    weights_refs, refs = refs[: len(which)], refs[len(which) :]
    pieces, refs = refs[:arrays], refs[arrays:]
    sums, refs = refs[: 2 * adds], refs[2 * adds :]
    own_ref, other_ref, weights, turned, values, weight_sems, sems = refs
    slots = len(plan)
    rows = own_ref.shape[0]
    length = own_ref.shape[1]
    step = pl.program_id(0)
    weight_copies = [
        pltpu.make_async_copy(weights_refs[s], weights.at[s], weight_sems.at[s])
        for s in range(len(which))
    ]
    copies = [
        [
            pltpu.make_async_copy(
                pieces[array].at[pl.ds(start, count)],
                values.at[s, pl.ds(target, count)],
                sems.at[5 * s + n],
            )
            for s in range(slots)
            for n, (array, start, count, target) in enumerate(plan[s])
            if target // length == q
        ]
        for q in range(4)
    ]

    @pl.when(step == 0)
    def _():
        for copy in weight_copies + copies[0] + copies[1] + copies[2] + copies[3]:
            copy.start()
        for copy in weight_copies:
            copy.wait()
        for s in range(slots):
            turned[s] = weights[at_ref[4 + s] - first].T

    for q in range(4):

        @pl.when(step == q)
        def _():
            for copy in copies[q]:
                copy.wait()
            total = None
            for s in range(slots):
                part = lax.dot_general(
                    turned[s],
                    values[s, q * length : (q + 1) * length],
                    (((1,), (1,)), ((), ())),
                    preferred_element_type=F32,
                )
                total = part if total is None else total + part
            own, other = total[:rows], total[rows:]
            if adds:
                own, other = own + sums[0][...], other + sums[1][...]
            own_ref[...] = own
            other_ref[...] = other.astype(other_ref.dtype)


def project_plain(slots, weights):
    total = 0.0
    for block, piece in zip(slots, weights):
        full = lax.all_gather(block, "ctx", axis=0, tiled=True)
        total = total + jnp.einsum("td,dc->ct", full, piece, preferred_element_type=F32)
    rows = total.shape[0] // 2
    return total[:rows], total[rows:]


def project(at, slots, weights, first, last, sums=(), send=F32):
    blocks, near, far = slots
    length, depth = blocks[0].shape
    half = length // 2
    rows = weights[0].shape[1] // 2
    arrays, plan = [], []

    def place_of(x):
        for n, y in enumerate(arrays):
            if y is x:
                return n
        arrays.append(x)
        return len(arrays) - 1

    for s in range(first, last):
        skip = (0, 0, length, half)[s]
        corner, row = ((2, 0), (2, half), (3, 0), (4, 0))[s]
        plan.append(
            (
                (place_of(blocks[s]), skip, length, 0),
                (place_of(near[s]), skip, length, length),
                (place_of(far[s]), skip, length, 2 * length),
                (place_of(near[corner]), row, half, 3 * length),
                (place_of(far[corner]), row, half, 3 * length + half),
            )
        )
    spec = pl.BlockSpec((rows, length), lambda g, at: (0, at[g]))
    return pl.pallas_call(
        functools.partial(project_kernel, plan, range(len(weights)), first, len(arrays), len(sums) // 2),
        grid_spec=pltpu.PrefetchScalarGridSpec(
            num_scalar_prefetch=1,
            grid=(4,),
            in_specs=[pl.BlockSpec(memory_space=pl.ANY)] * (len(weights) + len(arrays)) + [spec] * len(sums),
            out_specs=[spec] * 2,
            scratch_shapes=[
                pltpu.VMEM((len(weights), *weights[0].shape), BF16),
                pltpu.VMEM((last - first, 2 * rows, depth), BF16),
                pltpu.VMEM((last - first, 4 * length, depth), BF16),
                pltpu.SemaphoreType.DMA((len(weights),)),
                pltpu.SemaphoreType.DMA((5 * (last - first),)),
            ],
        ),
        out_shape=[
            jax.ShapeDtypeStruct((rows, 4 * length), F32),
            jax.ShapeDtypeStruct((rows, 4 * length), send),
        ],
        compiler_params=pltpu.CompilerParams(vmem_limit_bytes=PROJECT_LIMIT),
        name="project",
    )(at, *weights, *arrays, *sums)


def body(tokens, in_proj, short_taps, long_filter, skip_gain):
    length, depth = tokens.shape
    cycle = lax.axis_size("ctx")
    size = lax.axis_size("chan")
    chips = size // 2
    me = lax.axis_index("ctx")
    place = lax.axis_index("chan") // 2
    core = lax.axis_index("chan") % 2
    few = in_proj.shape[2] // (size * cycle)
    span = length * cycle
    high, low = (jnp.asarray(t) for t in wave_tables(length))
    pairs, singles = pick_columns(in_proj, chips, few, place, core, me, cycle)
    fits = cycle == 4 and chips == 4 and length % 512 == 0 and depth % 128 == 0
    own_taps = lax.dynamic_slice_in_dim(short_taps, me * few, few, axis=1)
    own_skip = lax.dynamic_slice_in_dim(skip_gain, me * few, few)[:, None]
    params = jnp.concatenate([own_taps[0], own_taps[1], own_taps[2], own_skip], axis=1)
    swapped = jnp.where((place == 1) | (place == 2), 1, 0)
    at = jnp.stack([me ^ q for q in range(4)] + [0 * me, 0 * me + 1, 2 + swapped, 3 - swapped])
    slots, pairs, singles, long_filter, (params, at) = (gather if fits else gather_plain)(
        tokens, pairs, singles, long_filter, (params, at.astype(jnp.int32))
    )
    moved_filter = lax.all_to_all(
        long_filter.reshape(cycle, few, length), "ctx", split_axis=0, concat_axis=0, tiled=True
    )
    if fits:
        slots, moved_filter = lax.optimization_barrier((slots, moved_filter))
        mine, send = project(at, slots, pairs, 0, 4)
        send, singles = lax.optimization_barrier((send, singles))
    else:
        mine, send = project_plain(slots, pairs)
    theirs = swap(send, "chan", 1)
    answer = convolve(
        mine.reshape(2, few, span), theirs.reshape(2, few, span), params, moved_filter, high, low
    )
    mine, send = project(at, slots, singles, 0, 4) if fits else project_plain(slots, singles)
    gated = gate(mine, swap(send, "chan", 1), params, answer, cycle)
    moved = lax.all_to_all(gated, "ctx", split_axis=0, concat_axis=0, tiled=True)
    return moved.reshape(cycle * few, length)


def solution(mesh):
    in_specs = (
        P("ctx", "chan"),
        P(None, "chan", None),
        P(None, "chan", None),
        P("chan", "ctx"),
        P("chan"),
    )
    out_specs = P("chan", "ctx")
    return jax.shard_map(body, mesh=mesh, in_specs=in_specs, out_specs=out_specs, check_vma=False)
```
